32 devices in a mesh: groups: 2 (over y), grid: 16 (over z, x, core).
Axes of the slice: x: 2, y: 2, z: 4, core: 2. Of those that a mesh axis runs over, the one named last changes fastest.
Arguments:
- tile_values: bfloat16 [1536, 4, 128, 128], P(('groups', 'grid')), parts along dimension 0, may hold values from -64 to 64
- tile_columns: int32 [192, 8, 4], P('groups'), parts along dimension 0, may hold values from 0 to 11, as said below
- keep_tiles: int32 [1536, 3], P(('groups', 'grid')), parts along dimension 0, may hold values 0 or 1
Outputs:
- inflated: float32 [1536, 3, 128, 128], P(('groups', 'grid')), parts along dimension 0
The draws below stay inside these ranges and needn't reach their ends.
There are 2 independent parts, one for each index of `groups`. The reference program is written for one: setup_inputs(seed, part) draws one part's arguments, and reference() takes and returns one part's arrays. A program takes and returns all parts, laid end to end along the dimension named above; each array names one. Nothing has to cross between parts.
Inputs may be any that keep to these rules, and one draw needn't show every extreme that they name: `tile_columns`: for each block row and column strip the 4 entries are distinct; at most 3 of them are below 3, and in every block of 48 block rows of one grid row, within each column strip, some block row has exactly 3 such entries.
All inputs are finite; a program needn't handle non-finite values. No bound on the sum of `keep_tiles` on one device may be relied on, other than what follows from the above.
Results may differ from the reference program's by a relative error of at most 0.0003.
Values may be sent and summed in bfloat16 or wider, within the bound.
No kernel may reach another device: no remote copies, remote signals or barrier semaphores. Data moves between devices by JAX's collectives and lax.ppermute only.
A program may use at most 256 MiB of HBM per device.

```python
import math
import jax
import jax.numpy as jnp
from jax import lax

TS = 128
GC = 8
CB = 12
WA = 4
W = 3
GR = 2
NB = 96
RB = 48
PC = 3
N_GRID = 16


def draw_tile_values(key, part):
    key = jax.random.fold_in(key, 11)
    key_noise, key_rows, key_cols = jax.random.split(key, 3)
    shape = (GR * GC * RB, WA, TS, TS)
    noise = jax.random.normal(key_noise, shape, jnp.float32)
    row_scale = jnp.exp(jax.random.uniform(key_rows, (GR * GC * RB, 1, TS, 1)) * math.log(10.0))
    col_scale = jnp.exp(jax.random.uniform(key_cols, (GR * GC * RB, WA, 1, TS)) * math.log(10.0))
    tier = (jnp.arange(GR * GC * RB) // (GC * RB)).astype(jnp.float32)
    rise = 1.0 + 2.0 * tier / max(GR - 1, 1)
    values = noise * row_scale * col_scale * rise[:, None, None, None] * 0.5
    return jnp.clip(values, -64.0, 64.0).astype(jnp.bfloat16)


def draw_tile_columns(key, part):
    key = jax.random.fold_in(key, 7)
    key_count, key_force, key_panel, key_other = jax.random.split(key, 4)
    taken = jax.random.randint(key_count, (NB, GC), 0, W + 1)
    chosen = jax.random.randint(key_force, (GR, 1, GC), 0, RB)
    local_rows = jnp.arange(RB)[None, :, None]
    forced = (local_rows == chosen).reshape(NB, GC)
    taken = jnp.where(forced, W, taken)
    panel_keys = jax.random.randint(key_panel, (NB, GC, PC), 0, 1 << 20) * PC + jnp.arange(PC)
    panel_order = jnp.argsort(panel_keys, axis=-1)
    other_keys = jax.random.randint(key_other, (NB, GC, CB - PC), 0, 1 << 20) * (CB - PC) + jnp.arange(CB - PC)
    other_order = jnp.argsort(other_keys, axis=-1) + PC
    places = jnp.arange(WA)
    panel_index = jnp.broadcast_to(jnp.minimum(places, PC - 1), (NB, GC, WA))
    from_panel = jnp.take_along_axis(panel_order, panel_index, axis=-1)
    other_index = jnp.clip(places[None, None, :] - taken[..., None], 0, CB - PC - 1)
    from_other = jnp.take_along_axis(other_order, other_index, axis=-1)
    return jnp.where(places[None, None, :] < taken[..., None], from_panel, from_other).astype(jnp.int32)


def with_ends(array, key, smallest, top_value):
    longest = array.shape.index(max(array.shape))
    spots = []
    for shift in (0, 1):
        where = [jax.random.randint(jax.random.fold_in(key, axis), (), 0, length) for axis, length in enumerate(array.shape)]
        where[longest] = (where[longest] + shift) % array.shape[longest]
        spots.append(tuple(where))
    return array.at[spots[0]].set(smallest).at[spots[1]].set(top_value)


def setup_inputs(seed: int = 0, part: int = 0) -> dict:
    splits = jax.random.split(jax.random.key(seed), 4)
    own_keys = jax.random.split(jax.random.fold_in(splits[3], part), 4)
    tile_values = draw_tile_values(jax.random.fold_in(jax.random.fold_in(splits[3], part), 71), part)
    tile_columns = draw_tile_columns(jax.random.fold_in(jax.random.fold_in(splits[3], part), 71), part)
    keep_tiles = with_ends((jax.random.randint(own_keys[2], (N_GRID * RB, PC), 0, 2) < 1).astype(jnp.int32), jax.random.fold_in(own_keys[2], 1), 0, 1)
    return {"tile_values": tile_values, "tile_columns": tile_columns, "keep_tiles": keep_tiles}


def reference(tile_values, tile_columns, keep_tiles):
    tiles = tile_values.reshape(GR, GC, RB, WA, TS, TS).transpose(0, 2, 1, 3, 4, 5).reshape(NB, GC, WA, TS, TS)
    matches = (tile_columns[..., None] == jnp.arange(PC, dtype=jnp.int32)).astype(jnp.float32)
    panel = jnp.einsum("rjtp,rjtab->rjpab", matches, tiles.astype(jnp.float32)).astype(jnp.bfloat16)
    columns = jnp.arange(GC, dtype=jnp.int32)[None, :, None] * CB + tile_columns

    def one_row(pair):
        row_tiles, row_columns = pair
        gathered = jnp.take(panel, row_columns, axis=0).astype(jnp.float32)
        return jnp.einsum("jtab,jtkpbc->kpac", row_tiles.astype(jnp.float32), gathered)

    expanded = lax.map(one_row, (tiles, columns))
    keep = keep_tiles.reshape(GR, GC, RB, PC).transpose(0, 2, 1, 3).reshape(NB, GC, PC).astype(jnp.float32)
    squared = expanded * expanded * keep[..., None, None]
    column_mean = jnp.sum(squared, axis=(0, 3)) / (NB * TS)
    inflated = squared / (column_mean[None, :, :, None, :] + 1e-6)
    return inflated.reshape(GR, RB, GC, PC, TS, TS).transpose(0, 2, 1, 3, 4, 5).reshape(GR * GC * RB, PC, TS, TS)
```

```python
import functools
import math

import jax
import jax.numpy as jnp
from jax import lax
from jax.experimental import pallas as pl
from jax.experimental.pallas import tpu as pltpu
from jax.sharding import PartitionSpec as P

GC = 8
CB = 12
PC = CB // 4
STRIPS = GC // 2
MIB = 1 << 20


def swapped(array, mask):
    return lax.ppermute(array, "grid", [(i, i ^ mask) for i in range(lax.axis_size("grid"))])


def panel_kernel(slot_ref, tiles_ref, panel_ref):
    rows, _, width, _ = tiles_ref.shape
    first = pl.program_id(0) * rows

    @pl.loop(0, rows)
    def _(r):
        for p in range(PC):
            slot = slot_ref[(first + r) * PC + p]
            tile = tiles_ref[r, jnp.maximum(slot, 0)]
            panel_ref[r, :, p * width : (p + 1) * width] = jnp.where(
                slot >= 0, tile, jnp.zeros_like(tile)
            )


def make_panel(tile_values, slots):
    block_rows, slots_per_row, width, _ = tile_values.shape
    step = math.gcd(block_rows, 12)
    return pl.pallas_call(
        panel_kernel,
        grid_spec=pltpu.PrefetchScalarGridSpec(
            num_scalar_prefetch=1,
            grid=(block_rows // step,),
            in_specs=[pl.BlockSpec((step, slots_per_row, width, width), lambda i, s: (i, 0, 0, 0))],
            out_specs=pl.BlockSpec((step, width, PC * width), lambda i, s: (i, 0, 0)),
        ),
        out_shape=jax.ShapeDtypeStruct((block_rows, width, PC * width), jnp.bfloat16),
        compiler_params=pltpu.CompilerParams(vmem_limit_bytes=40 * MIB),
        cost_estimate=pl.CostEstimate(flops=0, bytes_accessed=11_000_000, transcendentals=0),
        name="panel",
    )(slots.reshape(-1), tile_values)


def expand_kernel(chunks, parts, where_ref, index_ref, *refs):
    chunk_refs = refs[: chunks * STRIPS]
    panel_refs = refs[chunks * STRIPS : chunks * STRIPS + 2 * parts]
    mine_ref, other_ref, panel, tiles, sums, panel_sem, tile_sem, sum_sem = refs[
        chunks * STRIPS + 2 * parts :
    ]
    rows, slots, width, _ = chunk_refs[0].shape
    part_rows = panel_refs[0].shape[0]
    unit = math.gcd(CB, part_rows)
    units = CB // unit
    half = PC * width

    for q in range(STRIPS):
        for u in range(units):
            part = where_ref[2 * (q * units + u)]
            offset = where_ref[2 * (q * units + u) + 1]
            for n in range(parts):

                @pl.when(part == n)
                def _():
                    for side in range(2):
                        pltpu.make_async_copy(
                            panel_refs[side * parts + n].at[pl.ds(offset, unit)],
                            panel.at[
                                pl.ds(q * CB + u * unit, unit), :, pl.ds(side * half, half)
                            ],
                            panel_sem.at[side],
                        ).start()

    def fetch(k):
        return [
            pltpu.make_async_copy(
                chunk_refs[k * STRIPS + q], tiles.at[k % 2, q], tile_sem.at[k % 2, q]
            )
            for q in range(STRIPS)
        ]

    for copy in fetch(0):
        copy.start()
    for side in range(2):
        pltpu.make_async_copy(
            panel.at[:, :, pl.ds(side * half, half)],
            panel.at[:, :, pl.ds(side * half, half)],
            panel_sem.at[side],
        ).wait()

    def stores(row, slot):
        return [
            pltpu.make_async_copy(
                sums.at[slot, :, pl.ds(side * half, half)], out.at[row], sum_sem.at[slot, side]
            )
            for side, out in enumerate((mine_ref, other_ref))
        ]

    for k in range(chunks):
        if k + 1 < chunks:
            for copy in fetch(k + 1):
                copy.start()
        for copy in fetch(k):
            copy.wait()

        @pl.loop(0, rows)
        def _(r):
            row = k * rows + r
            slot = lax.rem(row, 2)

            @pl.when(row >= 2)
            def _():
                for copy in stores(row - 2, slot):
                    copy.wait()

            total = None
            for q in range(STRIPS):
                for t in range(0, slots, 2):
                    base = row * (STRIPS * slots) + q * slots + t
                    left = jnp.concatenate(
                        [tiles[k % 2, q, r, t], tiles[k % 2, q, r, t + 1]], axis=1
                    )
                    right = jnp.concatenate(
                        [panel[index_ref[base]], panel[index_ref[base + 1]]], axis=0
                    )
                    term = jnp.dot(left, right, preferred_element_type=jnp.float32)
                    total = term if total is None else total + term
            sums[slot] = total
            for copy in stores(row, slot):
                copy.start()

    for row in range(max(chunks * rows - 2, 0), chunks * rows):
        for copy in stores(row, row % 2):
            copy.wait()


def expand(chunk_list, panels, others, where, index):
    chunks = len(chunk_list)
    parts = len(panels)
    rows, slots, width, _ = chunk_list[0][0].shape
    total_rows = chunks * rows
    half = jax.ShapeDtypeStruct((total_rows, width, PC * width), jnp.float32)
    anywhere = pl.BlockSpec(memory_space=pl.ANY)
    smem = pl.BlockSpec(memory_space=pltpu.SMEM)
    operands = [a for chunk in chunk_list for a in chunk] + list(panels) + list(others)
    return pl.pallas_call(
        functools.partial(expand_kernel, chunks, parts),
        out_shape=(half, half),
        in_specs=[smem, smem] + [anywhere] * len(operands),
        out_specs=(anywhere, anywhere),
        scratch_shapes=[
            pltpu.VMEM((STRIPS * CB, width, 2 * PC * width), jnp.bfloat16),
            pltpu.VMEM((2, STRIPS, rows, slots, width, width), jnp.bfloat16),
            pltpu.VMEM((2, width, 2 * PC * width), jnp.float32),
            pltpu.SemaphoreType.DMA((2,)),
            pltpu.SemaphoreType.DMA((2, STRIPS)),
            pltpu.SemaphoreType.DMA((2, 2)),
        ],
        compiler_params=pltpu.CompilerParams(vmem_limit_bytes=48 * MIB),
        cost_estimate=pl.CostEstimate(
            flops=2 * total_rows * STRIPS * slots * width * width * 2 * PC * width * 2,
            bytes_accessed=30_000_000,
            transcendentals=0,
        ),
        name="expand",
    )(where, index.reshape(-1), *operands)


def square_kernel(keep_ref, mine_ref, got_ref, squared_ref, sums_ref):
    rows, width, _ = mine_ref.shape
    first = pl.program_id(0) * rows

    @pl.when(pl.program_id(0) == 0)
    def _():
        sums_ref[...] = jnp.zeros_like(sums_ref)

    @pl.loop(0, rows)
    def _(r):
        for p in range(PC):
            keep = keep_ref[(first + r) * PC + p].astype(jnp.float32)
            cols = slice(p * width, (p + 1) * width)
            value = mine_ref[r, :, cols] + got_ref[r, :, cols]
            value = value * value * keep
            squared_ref[r, :, cols] = value
            sums_ref[:, cols] += jnp.sum(value.reshape(width // 8, 8, width), axis=0)


def square(keep, mine, got):
    rows, width, half = mine.shape
    step = math.gcd(rows, 6)
    block = pl.BlockSpec((step, width, half), lambda i, s: (i, 0, 0))
    return pl.pallas_call(
        square_kernel,
        grid_spec=pltpu.PrefetchScalarGridSpec(
            num_scalar_prefetch=1,
            grid=(rows // step,),
            in_specs=[block, block],
            out_specs=(block, pl.BlockSpec((8, half), lambda i, s: (0, 0))),
        ),
        out_shape=(
            jax.ShapeDtypeStruct(mine.shape, jnp.float32),
            jax.ShapeDtypeStruct((8, half), jnp.float32),
        ),
        compiler_params=pltpu.CompilerParams(vmem_limit_bytes=40 * MIB),
        name="square",
    )(keep.reshape(-1), mine, got)


def scale_kernel(bounds, mean_ref, *refs):
    pieces, out_ref = refs[:-1], refs[-1]
    step, width, _ = pieces[0].shape
    at = pl.program_id(0) * step
    for n, piece in enumerate(pieces):

        @pl.when((at >= bounds[n]) & (at < bounds[n + 1]))
        def _():
            for p in range(PC):
                cols = slice(p * width, (p + 1) * width)
                inverse = 1.0 / (mean_ref[0:1, cols] + 1e-6)
                for r in range(step):
                    out_ref[r, p] = piece[r, :, cols] * inverse


def scale(mean, pieces):
    _, width, half = pieces[0].shape
    step = functools.reduce(math.gcd, [p.shape[0] for p in pieces])
    bounds = [0]
    for p in pieces:
        bounds.append(bounds[-1] + p.shape[0])

    def block_of(n):
        low, count = bounds[n] // step, pieces[n].shape[0] // step
        return pl.BlockSpec(
            (step, width, half), lambda i: (jnp.clip(i - low, 0, count - 1), 0, 0)
        )

    return pl.pallas_call(
        functools.partial(scale_kernel, tuple(bounds)),
        grid=(bounds[-1] // step,),
        in_specs=[pl.BlockSpec((1, half), lambda i: (0, 0))]
        + [block_of(n) for n in range(len(pieces))],
        out_specs=pl.BlockSpec((step, PC, width, width), lambda i: (i, 0, 0, 0)),
        out_shape=jax.ShapeDtypeStruct((bounds[-1], PC, width, width), jnp.float32),
        compiler_params=pltpu.CompilerParams(vmem_limit_bytes=48 * MIB),
        name="scale",
    )(mean, *pieces)


class Lane:
    def __init__(self, window):
        self.window = window
        self.sent = []

    def send(self, array, mask):
        if len(self.sent) >= self.window:
            array, _ = lax.optimization_barrier((array, self.sent[-self.window]))
        out = swapped(array, mask)
        self.sent.append(out)
        return out


def shards(tile_values, tile_columns, keep_tiles):
    devices = lax.axis_size("grid")
    device = lax.axis_index("grid")
    all_bits = devices.bit_length() - 1
    low_bits = GC.bit_length() - 1
    row_strip = device // GC
    col_strip = device % GC
    block_rows, slots, width, _ = tile_values.shape
    chunks = math.gcd(block_rows, 8)
    rows = block_rows // chunks

    strip_rows = lax.dynamic_slice_in_dim(tile_columns, row_strip * block_rows, block_rows, 0)
    strips = jnp.bitwise_xor(col_strip, 2 * jnp.arange(STRIPS, dtype=jnp.int32))
    pattern = jnp.take(strip_rows, strips, axis=1)
    own = pattern[:, 0]
    match = own[:, :, None] == jnp.arange(PC, dtype=jnp.int32)
    slot = jnp.max(
        jnp.where(match, jnp.arange(slots, dtype=jnp.int32)[None, :, None], -1), axis=1
    )
    index = pattern + CB * jnp.arange(STRIPS, dtype=jnp.int32)[None, :, None]
    index = index.reshape(block_rows, STRIPS * slots)
    unit = math.gcd(CB, block_rows)
    unit_rows = strips[:, None] * CB + unit * jnp.arange(CB // unit, dtype=jnp.int32)
    where = jnp.stack(
        [jnp.bitwise_xor(unit_rows // block_rows, row_strip), unit_rows % block_rows], axis=-1
    ).reshape(-1)

    panels = [make_panel(tile_values, slot)]
    for bit in range(low_bits, all_bits):
        panels = panels + [swapped(p, 1 << bit) for p in panels]
    others = [swapped(p, 1) for p in panels]

    own_chunks = [lax.slice_in_dim(tile_values, k * rows, (k + 1) * rows) for k in range(chunks)]
    x_lane, z_lane = Lane(2), Lane(2)
    from_x, from_z, from_xz = [], [], []
    for k in range(chunks):
        from_x.append(x_lane.send(own_chunks[k], 2))
        from_z.append(z_lane.send(own_chunks[k], 4))
        if k > 0:
            from_xz.append(x_lane.send(from_z[k - 1], 2))
    from_xz.append(z_lane.send(from_x[chunks - 1], 4))

    squares, sums = [], []
    first = 0
    for count in (chunks - 3, 2, 1) if chunks > 3 else (chunks,):
        ks = range(first, first + count)
        lo, hi = first * rows, (first + count) * rows
        mine, other = expand(
            [(own_chunks[k], from_x[k], from_z[k], from_xz[k]) for k in ks],
            panels,
            others,
            where,
            index[lo:hi],
        )
        squared, total = square(keep_tiles[lo:hi], mine, swapped(other, 1))
        squares.append(squared)
        sums.append(jnp.sum(total, axis=0, keepdims=True))
        first += count
    column_sums = functools.reduce(jnp.add, sums)
    for bit in range(low_bits, all_bits):
        column_sums = column_sums + swapped(column_sums, 1 << bit)
    column_mean = column_sums / (CB * GC * width)
    return scale(column_mean, squares)


def solution(mesh):
    return jax.shard_map(
        shards,
        mesh=mesh,
        in_specs=(
            P(("groups", "grid"), None, None, None),
            P("groups", None, None),
            P(("groups", "grid"), None),
        ),
        out_specs=P(("groups", "grid"), None, None, None),
        check_vma=False,
    )
```

```python
import functools
import math

import jax
import jax.numpy as jnp
from jax import lax
from jax.experimental import pallas as pl
from jax.experimental.pallas import tpu as pltpu
from jax.sharding import PartitionSpec as P

GC = 8
CB = 12
PC = CB // 4
STRIPS = GC // 2
MIB = 1 << 20


def swapped(array, mask):
    return lax.ppermute(array, "grid", [(i, i ^ mask) for i in range(lax.axis_size("grid"))])


def panel_kernel(slot_ref, tiles_ref, panel_ref):
    rows, _, width, _ = tiles_ref.shape
    first = pl.program_id(0) * rows

    @pl.loop(0, rows)
    def _(r):
        for p in range(PC):
            slot = slot_ref[(first + r) * PC + p]
            tile = tiles_ref[r, jnp.maximum(slot, 0)]
            panel_ref[r, :, p * width : (p + 1) * width] = jnp.where(
                slot >= 0, tile, jnp.zeros_like(tile)
            )


def make_panel(tile_values, slots):
    block_rows, slots_per_row, width, _ = tile_values.shape
    step = math.gcd(block_rows, 12)
    return pl.pallas_call(
        panel_kernel,
        grid_spec=pltpu.PrefetchScalarGridSpec(
            num_scalar_prefetch=1,
            grid=(block_rows // step,),
            in_specs=[pl.BlockSpec((step, slots_per_row, width, width), lambda i, s: (i, 0, 0, 0))],
            out_specs=pl.BlockSpec((step, width, PC * width), lambda i, s: (i, 0, 0)),
        ),
        out_shape=jax.ShapeDtypeStruct((block_rows, width, PC * width), jnp.bfloat16),
        compiler_params=pltpu.CompilerParams(vmem_limit_bytes=40 * MIB),
        cost_estimate=pl.CostEstimate(flops=0, bytes_accessed=11_000_000, transcendentals=0),
        name="panel",
    )(slots.reshape(-1), tile_values)


def pack_kernel(first, parts, where_ref, *refs):
    sources, packed_ref, sem = refs[: 2 * parts], refs[-2], refs[-1]
    part_rows, _, half = sources[0].shape
    unit = math.gcd(CB, part_rows)
    for n in range(packed_ref.shape[0] // unit):
        part = where_ref[2 * (first + n)]
        offset = where_ref[2 * (first + n) + 1]
        for m in range(parts):

            @pl.when((part == m) | (parts == 1))
            def _():
                for side in range(2):
                    pltpu.make_async_copy(
                        sources[side * parts + m].at[pl.ds(offset, unit)],
                        packed_ref.at[pl.ds(n * unit, unit), :, pl.ds(side * half, half)],
                        sem.at[side],
                    ).start()
    for side in range(2):
        cols = pl.ds(side * half, half)
        pltpu.make_async_copy(
            packed_ref.at[:, :, cols], packed_ref.at[:, :, cols], sem.at[side]
        ).wait()


def pack(where, first, mine, others):
    parts = len(mine)
    _, width, half = mine[0].shape
    return pl.pallas_call(
        functools.partial(pack_kernel, first, parts),
        out_shape=jax.ShapeDtypeStruct((STRIPS // 2 * CB, width, 2 * half), jnp.bfloat16),
        in_specs=[pl.BlockSpec(memory_space=pltpu.SMEM)]
        + [pl.BlockSpec(memory_space=pl.ANY)] * (2 * parts),
        out_specs=pl.BlockSpec(memory_space=pltpu.VMEM),
        scratch_shapes=[pltpu.SemaphoreType.DMA((2,))],
        compiler_params=pltpu.CompilerParams(vmem_limit_bytes=16 * MIB),
        cost_estimate=pl.CostEstimate(flops=0, bytes_accessed=8_000_000, transcendentals=0),
        name="pack",
    )(where, *mine, *others)


def expand_kernel(chunks, order_ref, index_ref, near_ref, far_ref, *refs):
    chunk_refs = refs[: chunks * STRIPS]
    mine_ref, other_ref, tiles, sums, tile_sem, sum_sem = refs[chunks * STRIPS :]
    rows, slots, width, _ = chunk_refs[0].shape
    half = PC * width

    def fetch(k):
        return [
            pltpu.make_async_copy(
                chunk_refs[k * STRIPS + q], tiles.at[k % 2, q], tile_sem.at[k % 2, q]
            )
            for q in range(STRIPS)
        ]

    for copy in fetch(0):
        copy.start()

    def stores(row, slot):
        return [
            pltpu.make_async_copy(
                sums.at[slot, :, pl.ds(side * half, half)], out.at[row], sum_sem.at[slot, side]
            )
            for side, out in enumerate((mine_ref, other_ref))
        ]

    for k in range(chunks):
        if k + 1 < chunks:
            for copy in fetch(k + 1):
                copy.start()
        for copy in fetch(k):
            copy.wait()

        @pl.loop(0, rows)
        def _(r):
            row = k * rows + r
            slot = lax.rem(row, 2)

            @pl.when(row >= 2)
            def _():
                for copy in stores(row - 2, slot):
                    copy.wait()

            total = None
            for n in range(STRIPS):
                panel = near_ref if n < STRIPS // 2 else far_ref
                q = order_ref[n]
                for t in range(0, slots, 2):
                    base = row * (STRIPS * slots) + n * slots + t
                    left = jnp.concatenate(
                        [tiles[k % 2, q, r, t], tiles[k % 2, q, r, t + 1]], axis=1
                    )
                    right = jnp.concatenate(
                        [panel[index_ref[base]], panel[index_ref[base + 1]]], axis=0
                    )
                    term = jnp.dot(left, right, preferred_element_type=jnp.float32)
                    total = term if total is None else total + term
            sums[slot] = total
            for copy in stores(row, slot):
                copy.start()

    for row in range(max(chunks * rows - 2, 0), chunks * rows):
        for copy in stores(row, row % 2):
            copy.wait()


def expand(chunk_list, order, index, near, far):
    chunks = len(chunk_list)
    rows, slots, width, _ = chunk_list[0][0].shape
    total_rows = chunks * rows
    half = jax.ShapeDtypeStruct((total_rows, width, PC * width), jnp.float32)
    anywhere = pl.BlockSpec(memory_space=pltpu.HBM)
    smem = pl.BlockSpec(memory_space=pltpu.SMEM)
    vmem = pl.BlockSpec(memory_space=pltpu.VMEM)
    operands = [a for chunk in chunk_list for a in chunk]
    return pl.pallas_call(
        functools.partial(expand_kernel, chunks),
        out_shape=(half, half),
        in_specs=[smem, smem, vmem, vmem] + [anywhere] * len(operands),
        out_specs=(anywhere, anywhere),
        scratch_shapes=[
            pltpu.VMEM((2, STRIPS, rows, slots, width, width), jnp.bfloat16),
            pltpu.VMEM((2, width, 2 * PC * width), jnp.float32),
            pltpu.SemaphoreType.DMA((2, STRIPS)),
            pltpu.SemaphoreType.DMA((2, 2)),
        ],
        compiler_params=pltpu.CompilerParams(vmem_limit_bytes=24 * MIB),
        cost_estimate=pl.CostEstimate(
            flops=2 * total_rows * STRIPS * slots * width * width * 2 * PC * width * 2,
            bytes_accessed=30_000_000,
            transcendentals=0,
        ),
        name="expand",
    )(order, index.reshape(-1), near, far, *operands)


def square_kernel(keep_ref, before_ref, mine_ref, got_ref, squared_ref, sums_ref):
    rows, width, _ = mine_ref.shape
    first = pl.program_id(0) * rows

    @pl.when(pl.program_id(0) == 0)
    def _():
        sums_ref[...] = before_ref[...]

    @pl.loop(0, rows)
    def _(r):
        for p in range(PC):
            keep = keep_ref[(first + r) * PC + p].astype(jnp.float32)
            cols = slice(p * width, (p + 1) * width)
            value = mine_ref[r, :, cols] + got_ref[r, :, cols]
            value = value * value * keep
            squared_ref[r, :, cols] = value
            sums_ref[:, cols] += jnp.sum(value.reshape(width // 8, 8, width), axis=0)


def square(keep, before, mine, got):
    rows, width, half = mine.shape
    step = math.gcd(rows, 6)
    block = pl.BlockSpec((step, width, half), lambda i, s: (i, 0, 0))
    sums = pl.BlockSpec((8, half), lambda i, s: (0, 0))
    return pl.pallas_call(
        square_kernel,
        grid_spec=pltpu.PrefetchScalarGridSpec(
            num_scalar_prefetch=1,
            grid=(rows // step,),
            in_specs=[sums, block, block],
            out_specs=(block, sums),
        ),
        out_shape=(
            jax.ShapeDtypeStruct(mine.shape, jnp.float32),
            jax.ShapeDtypeStruct((8, half), jnp.float32),
        ),
        compiler_params=pltpu.CompilerParams(vmem_limit_bytes=24 * MIB),
        cost_estimate=pl.CostEstimate(
            flops=0, bytes_accessed=3 * mine.size * 4, transcendentals=0
        ),
        name="square",
    )(keep.reshape(-1), before, mine, got)


def scale_kernel(bounds, count, sums_ref, got_ref, *refs):
    pieces, out_ref = refs[:-1], refs[-1]
    step, width, _ = pieces[0].shape
    at = pl.program_id(0) * step
    for n, piece in enumerate(pieces):

        @pl.when((at >= bounds[n]) & (at < bounds[n + 1]))
        def _():
            for p in range(PC):
                cols = slice(p * width, (p + 1) * width)
                sums = jnp.sum(sums_ref[:, cols] + got_ref[:, cols], axis=0, keepdims=True)
                inverse = 1.0 / (sums / count + 1e-6)
                for r in range(step):
                    out_ref[r, p] = piece[r, :, cols] * inverse


def scale(count, sums, got, pieces):
    _, width, half = pieces[0].shape
    step = functools.reduce(math.gcd, [p.shape[0] for p in pieces])
    bounds = [0]
    for p in pieces:
        bounds.append(bounds[-1] + p.shape[0])

    def block_of(n):
        low, number = bounds[n] // step, pieces[n].shape[0] // step
        return pl.BlockSpec(
            (step, width, half), lambda i: (jnp.clip(i - low, 0, number - 1), 0, 0)
        )

    return pl.pallas_call(
        functools.partial(scale_kernel, tuple(bounds), count),
        grid=(bounds[-1] // step,),
        in_specs=[pl.BlockSpec((8, half), lambda i: (0, 0))] * 2
        + [block_of(n) for n in range(len(pieces))],
        out_specs=pl.BlockSpec((step, PC, width, width), lambda i: (i, 0, 0, 0)),
        out_shape=jax.ShapeDtypeStruct((bounds[-1], PC, width, width), jnp.float32),
        compiler_params=pltpu.CompilerParams(vmem_limit_bytes=40 * MIB),
        name="scale",
    )(sums, got, *pieces)


def after(array, *earlier):
    return lax.optimization_barrier((array, *earlier))[0]


class Lane:
    def __init__(self, window):
        self.window = window
        self.sent = []

    def send(self, array, mask):
        if len(self.sent) >= self.window:
            array = after(array, self.sent[-self.window])
        out = swapped(array, mask)
        self.sent.append(out)
        return out


def shards(tile_values, tile_columns, keep_tiles):
    devices = lax.axis_size("grid")
    device = lax.axis_index("grid")
    all_bits = devices.bit_length() - 1
    low_bits = GC.bit_length() - 1
    grid_rows = devices // GC
    row_strip = device // GC
    col_strip = device % GC
    block_rows, slots, width, _ = tile_values.shape
    chunks = math.gcd(block_rows, 8)
    rows = block_rows // chunks
    pair = STRIPS // 2

    strip_rows = lax.dynamic_slice_in_dim(tile_columns, row_strip * block_rows, block_rows, 0)
    far_first = 0
    if block_rows == pair * 2 * CB:
        far_first = pair * (col_strip // (pair * 2) != row_strip).astype(jnp.int32)
    order = jnp.bitwise_xor(jnp.arange(STRIPS, dtype=jnp.int32), far_first)
    strips = jnp.bitwise_xor(col_strip, 2 * order)
    own = jnp.take(strip_rows, col_strip, axis=1)
    match = own[:, :, None] == jnp.arange(PC, dtype=jnp.int32)
    slot = jnp.max(
        jnp.where(match, jnp.arange(slots, dtype=jnp.int32)[None, :, None], -1), axis=1
    )
    index = jnp.take(strip_rows, strips, axis=1)
    index = index + CB * (jnp.arange(STRIPS, dtype=jnp.int32) % pair)[None, :, None]
    index = index.reshape(block_rows, STRIPS * slots)
    unit = math.gcd(CB, block_rows)
    unit_rows = strips[:, None] * CB + unit * jnp.arange(CB // unit, dtype=jnp.int32)
    where = jnp.stack(
        [jnp.bitwise_xor(unit_rows // block_rows, row_strip), unit_rows % block_rows], axis=-1
    ).reshape(-1)

    own_chunks = [lax.slice_in_dim(tile_values, k * rows, (k + 1) * rows) for k in range(chunks)]
    x_lane, z_lane = Lane(2), Lane(1)
    from_x, from_z, from_xz = [], [], []
    for k in range(chunks):
        from_x.append(x_lane.send(own_chunks[k], 2))
        from_z.append(z_lane.send(own_chunks[k], 4))
        if k > 1:
            from_xz.append(x_lane.send(from_z[k - 2], 2))
    from_xz.append(x_lane.send(from_z[chunks - 2], 2))
    from_xz.append(z_lane.send(from_x[chunks - 1], 4))

    panels = [make_panel(tile_values, slot)]
    for bit in range(low_bits, all_bits):
        panels = panels + [swapped(p, 1 << bit) for p in panels]
    half = len(where) // 2
    if block_rows == pair * 2 * CB and grid_rows == 2:
        near_other = swapped(panels[0], 1)
        near = pack(where, 0, panels[:1], [near_other])
        far_mine = after(panels[1], from_x[-1], from_z[-1], from_xz[-4])
        far = pack(where, half // 2, [far_mine], [swapped(far_mine, 1)])
    else:
        others = [swapped(p, 1) for p in panels]
        near = pack(where, 0, panels, others)
        far = pack(where, half // 2, panels, others)

    squares = []
    sums = jnp.zeros((8, PC * width), jnp.float32)
    first = 0
    for count in (chunks - 2, 2) if chunks > 3 else (chunks,):
        ks = range(first, first + count)
        lo, hi = first * rows, (first + count) * rows
        mine, other = expand(
            [(own_chunks[k], from_x[k], from_z[k], from_xz[k]) for k in ks],
            order,
            index[lo:hi],
            near,
            far,
        )
        squared, sums = square(keep_tiles[lo:hi], sums, mine, swapped(other, 1))
        squares.append(squared)
        first += count
    for bit in range(low_bits, all_bits - 1):
        sums = sums + swapped(sums, 1 << bit)
    got = swapped(sums, 1 << (all_bits - 1))
    return scale(float(CB * GC * width), sums, got, squares)


def solution(mesh):
    return jax.shard_map(
        shards,
        mesh=mesh,
        in_specs=(
            P(("groups", "grid"), None, None, None),
            P("groups", None, None),
            P(("groups", "grid"), None),
        ),
        out_specs=P(("groups", "grid"), None, None, None),
        check_vma=False,
    )
```

```python
import functools
import math

import jax
import jax.numpy as jnp
from jax import lax
from jax.experimental import pallas as pl
from jax.experimental.pallas import tpu as pltpu
from jax.sharding import PartitionSpec as P

GC = 8
CB = 12
PC = CB // 4
STRIPS = GC // 2
MIB = 1 << 20
SHORT = pl.CostEstimate(flops=0, bytes_accessed=1024, transcendentals=0)


def swapped(array, mask, among=lambda i: True):
    pairs = [(i, i ^ mask) for i in range(lax.axis_size("grid")) if among(i)]
    return lax.ppermute(array, "grid", pairs)


def inner(i):
    return (i ^ i >> 1) & (GC // 2) != 0


def panel_kernel(slot_ref, tiles_ref, panel_ref):
    rows, _, width, _ = tiles_ref.shape
    first = pl.program_id(0) * rows

    @pl.loop(0, rows)
    def _(r):
        for p in range(PC):
            slot = slot_ref[(first + r) * PC + p]
            tile = tiles_ref[r, jnp.maximum(slot, 0)]
            panel_ref[r, :, p * width : (p + 1) * width] = jnp.where(
                slot >= 0, tile, jnp.zeros_like(tile)
            )


def make_panel(tile_values, slots):
    block_rows, slots_per_row, width, _ = tile_values.shape
    step = math.gcd(block_rows, 12)
    return pl.pallas_call(
        panel_kernel,
        grid_spec=pltpu.PrefetchScalarGridSpec(
            num_scalar_prefetch=1,
            grid=(block_rows // step,),
            in_specs=[pl.BlockSpec((step, slots_per_row, width, width), lambda i, s: (i, 0, 0, 0))],
            out_specs=pl.BlockSpec((step, width, PC * width), lambda i, s: (i, 0, 0)),
        ),
        out_shape=jax.ShapeDtypeStruct((block_rows, width, PC * width), jnp.bfloat16),
        compiler_params=pltpu.CompilerParams(vmem_limit_bytes=12 * MIB),
        cost_estimate=SHORT,
        name="panel",
    )(slots.reshape(-1), tile_values)


def pack_kernel(first, parts, where_ref, *refs):
    sources, packed_ref, sem = refs[: 2 * parts], refs[-2], refs[-1]
    part_rows, _, half = sources[0].shape
    unit = math.gcd(CB, part_rows)
    for n in range(packed_ref.shape[0] // unit):
        part = where_ref[2 * (first + n)]
        offset = where_ref[2 * (first + n) + 1]
        for m in range(parts):

            @pl.when((part == m) | (parts == 1))
            def _():
                for side in range(2):
                    pltpu.make_async_copy(
                        sources[side * parts + m].at[pl.ds(offset, unit)],
                        packed_ref.at[pl.ds(n * unit, unit), :, pl.ds(side * half, half)],
                        sem.at[side],
                    ).start()
    for side in range(2):
        cols = pl.ds(side * half, half)
        pltpu.make_async_copy(
            packed_ref.at[:, :, cols], packed_ref.at[:, :, cols], sem.at[side]
        ).wait()


def pack(where, first, mine, others):
    parts = len(mine)
    _, width, half = mine[0].shape
    return pl.pallas_call(
        functools.partial(pack_kernel, first, parts),
        out_shape=jax.ShapeDtypeStruct((STRIPS // 2 * CB, width, 2 * half), jnp.bfloat16),
        in_specs=[pl.BlockSpec(memory_space=pltpu.SMEM)]
        + [pl.BlockSpec(memory_space=pl.ANY)] * (2 * parts),
        out_specs=pl.BlockSpec(memory_space=pltpu.VMEM),
        scratch_shapes=[pltpu.SemaphoreType.DMA((2,))],
        compiler_params=pltpu.CompilerParams(vmem_limit_bytes=8 * MIB),
        cost_estimate=SHORT,
        name="pack",
    )(where, *mine, *others)


def expand_kernel(offsets, order_ref, index_ref, near_ref, far_ref, *refs):
    tile_refs = refs[:STRIPS]
    mine_ref, other_ref, tiles, sums, tile_sem, sum_sem = refs[STRIPS:]
    _, _, rows, slots, width, _ = tiles.shape
    half = PC * width
    total_rows = mine_ref.shape[0]
    steps = total_rows // rows

    def fetch(k):
        return [
            pltpu.make_async_copy(
                source.at[pl.ds(offset + k * rows, rows)], tiles.at[k % 2, q], tile_sem.at[k % 2, q]
            )
            for q, (source, offset) in enumerate(zip(tile_refs, offsets))
        ]

    def stores(row, slot):
        return [
            pltpu.make_async_copy(
                sums.at[slot, :, pl.ds(side * half, half)], out.at[row], sum_sem.at[slot, side]
            )
            for side, out in enumerate((mine_ref, other_ref))
        ]

    for copy in fetch(0):
        copy.start()
    for k in range(steps):
        if k + 1 < steps:
            for copy in fetch(k + 1):
                copy.start()
        for copy in fetch(k):
            copy.wait()

        @pl.loop(0, rows)
        def _(r):
            row = k * rows + r
            slot = lax.rem(row, 2)

            @pl.when(row >= 2)
            def _():
                for copy in stores(row - 2, slot):
                    copy.wait()

            total = None
            for n in range(STRIPS):
                panel = near_ref if n < STRIPS // 2 else far_ref
                q = order_ref[n]
                for t in range(0, slots, 2):
                    base = row * (STRIPS * slots) + n * slots + t
                    left = jnp.concatenate(
                        [tiles[k % 2, q, r, t], tiles[k % 2, q, r, t + 1]], axis=1
                    )
                    right = jnp.concatenate(
                        [panel[index_ref[base]], panel[index_ref[base + 1]]], axis=0
                    )
                    term = jnp.dot(left, right, preferred_element_type=jnp.float32)
                    total = term if total is None else total + term
            sums[slot] = total
            for copy in stores(row, slot):
                copy.start()

    for row in range(max(total_rows - 2, 0), total_rows):
        for copy in stores(row, row % 2):
            copy.wait()


def expand(sources, order, index, near, far):
    arrays, offsets = zip(*sources)
    _, slots, width, _ = arrays[0].shape
    total_rows = index.shape[0]
    rows = math.gcd(total_rows, 6)
    half = jax.ShapeDtypeStruct((total_rows, width, PC * width), jnp.float32)
    anywhere = pl.BlockSpec(memory_space=pl.ANY)
    smem = pl.BlockSpec(memory_space=pltpu.SMEM)
    vmem = pl.BlockSpec(memory_space=pltpu.VMEM)
    return pl.pallas_call(
        functools.partial(expand_kernel, offsets),
        out_shape=(half, half),
        in_specs=[smem, smem, vmem, vmem] + [anywhere] * STRIPS,
        out_specs=(anywhere, anywhere),
        scratch_shapes=[
            pltpu.VMEM((2, STRIPS, rows, slots, width, width), jnp.bfloat16),
            pltpu.VMEM((2, width, 2 * PC * width), jnp.float32),
            pltpu.SemaphoreType.DMA((2, STRIPS)),
            pltpu.SemaphoreType.DMA((2, 2)),
        ],
        compiler_params=pltpu.CompilerParams(vmem_limit_bytes=12 * MIB),
        cost_estimate=SHORT,
        name="expand",
    )(order, index.reshape(-1), near, far, *arrays)


def square_kernel(keep_ref, before_ref, mine_ref, got_ref, *refs):
    squared_ref, sums_ref = refs[-2:]
    rows, width, _ = mine_ref.shape
    first = pl.program_id(0) * rows

    @pl.when(pl.program_id(0) == 0)
    def _():
        sums_ref[...] = before_ref[...]

    @pl.loop(0, rows)
    def _(r):
        for p in range(PC):
            keep = keep_ref[(first + r) * PC + p].astype(jnp.float32)
            cols = slice(p * width, (p + 1) * width)
            value = mine_ref[r, :, cols] + got_ref[r, :, cols]
            value = value * value * keep
            squared_ref[r, :, cols] = value
            sums_ref[:, cols] += jnp.sum(value.reshape(width // 8, 8, width), axis=0)


def square(keep, before, mine, got, lo, total_rows, buffer):
    rows, width, half = mine.shape
    step = math.gcd(math.gcd(rows, 6), lo) if lo else math.gcd(rows, 6)
    block = pl.BlockSpec((step, width, half), lambda i, s: (i, 0, 0))
    target = pl.BlockSpec((step, width, half), lambda i, s: (lo // step + i, 0, 0))
    sums = pl.BlockSpec((8, half), lambda i, s: (0, 0))
    operands = [keep.reshape(-1), before, mine, got]
    in_specs = [sums, block, block]
    aliases = {}
    if buffer is not None:
        operands.append(buffer)
        in_specs.append(pl.BlockSpec(memory_space=pl.ANY))
        aliases = {len(operands) - 1: 0}
    return pl.pallas_call(
        square_kernel,
        grid_spec=pltpu.PrefetchScalarGridSpec(
            num_scalar_prefetch=1,
            grid=(rows // step,),
            in_specs=in_specs,
            out_specs=(target, sums),
        ),
        out_shape=(
            jax.ShapeDtypeStruct((total_rows, width, half), jnp.float32),
            jax.ShapeDtypeStruct((8, half), jnp.float32),
        ),
        input_output_aliases=aliases,
        compiler_params=pltpu.CompilerParams(vmem_limit_bytes=12 * MIB),
        cost_estimate=SHORT,
        name="square",
    )(*operands)


def scale_kernel(count, sums_ref, got_ref, squared_ref, out_ref):
    step, width, _ = squared_ref.shape
    for p in range(PC):
        cols = slice(p * width, (p + 1) * width)
        sums = jnp.sum(sums_ref[:, cols] + got_ref[:, cols], axis=0, keepdims=True)
        inverse = 1.0 / (sums / count + 1e-6)
        for r in range(step):
            out_ref[r, p] = squared_ref[r, :, cols] * inverse


def scale(count, sums, got, squared):
    rows, width, half = squared.shape
    step = math.gcd(rows, 6)
    return pl.pallas_call(
        functools.partial(scale_kernel, count),
        grid=(rows // step,),
        in_specs=[pl.BlockSpec((8, half), lambda i: (0, 0))] * 2
        + [pl.BlockSpec((step, width, half), lambda i: (i, 0, 0))],
        out_specs=pl.BlockSpec((step, PC, width, width), lambda i: (i, 0, 0, 0)),
        out_shape=jax.ShapeDtypeStruct((rows, PC, width, width), jnp.float32),
        compiler_params=pltpu.CompilerParams(vmem_limit_bytes=12 * MIB),
        cost_estimate=SHORT,
        name="scale",
    )(sums, got, squared)


def after(array, *earlier):
    return lax.optimization_barrier((array, *earlier))[0]


def shards(tile_values, tile_columns, keep_tiles):
    devices = lax.axis_size("grid")
    device = lax.axis_index("grid")
    all_bits = devices.bit_length() - 1
    low_bits = GC.bit_length() - 1
    grid_rows = devices // GC
    row_strip = device // GC
    col_strip = device % GC
    block_rows, slots, width, _ = tile_values.shape
    pair = STRIPS // 2

    strip_rows = lax.dynamic_slice_in_dim(tile_columns, row_strip * block_rows, block_rows, 0)
    far_first = 0
    if block_rows == pair * 2 * CB:
        far_first = pair * (col_strip // (pair * 2) != row_strip).astype(jnp.int32)
    order = jnp.bitwise_xor(jnp.arange(STRIPS, dtype=jnp.int32), far_first)
    strips = jnp.bitwise_xor(col_strip, 2 * order)
    own = jnp.take(strip_rows, col_strip, axis=1)
    match = own[:, :, None] == jnp.arange(PC, dtype=jnp.int32)
    slot = jnp.max(
        jnp.where(match, jnp.arange(slots, dtype=jnp.int32)[None, :, None], -1), axis=1
    )
    index = jnp.take(strip_rows, strips, axis=1)
    index = index + CB * (jnp.arange(STRIPS, dtype=jnp.int32) % pair)[None, :, None]
    index = index.reshape(block_rows, STRIPS * slots)
    relayed = grid_rows == 2 and block_rows == 2 * pair * CB
    unit = math.gcd(CB, block_rows)
    unit_rows = strips[:, None] * CB + unit * jnp.arange(CB // unit, dtype=jnp.int32)
    part = jnp.bitwise_xor(unit_rows // block_rows, row_strip)
    offset = unit_rows % block_rows
    if relayed:
        part, offset = offset // (2 * CB), offset % CB
    where = jnp.stack([part, offset], axis=-1).reshape(-1)
    half = len(where) // 2

    def shared(pieces):
        odd = col_strip % 2 == 1
        pieces = [p[r : r + CB] for p in pieces for r in range(0, p.shape[0], CB)]
        kept = [jnp.where(odd, b, a) for a, b in zip(pieces[::2], pieces[1::2])]
        given = [jnp.where(odd, a, b) for a, b in zip(pieces[::2], pieces[1::2])]
        return kept, [swapped(p, 1) for p in given]

    cuts = [0, 3 * block_rows // 8, 2 * (3 * block_rows // 8), block_rows]
    parts = list(zip(cuts[:-1], cuts[1:]))
    own = [tile_values[lo:hi] for lo, hi in parts]
    panel = make_panel(tile_values, slot)
    from_x = swapped(tile_values, 2)
    from_z = [swapped(own[0], 4)]
    if relayed:
        step = block_rows // 2
        is_inner = inner(device)
        pieces = [panel[:step], panel[step:]]
        near = pack(where, 0, *shared(pieces))
        across = GC + GC // 2
        crossed = [swapped(pieces[0], across, inner)]
        crossed.append(swapped(after(pieces[1], crossed[0]), across, inner))
        passed = []
        for got, piece in zip(crossed, pieces):
            got = after(got, *(passed or from_z))
            passed.append(swapped(jnp.where(is_inner, got, piece), 4))
        returned = [swapped(after(passed[0], crossed[1]), across, inner)]
        returned.append(swapped(after(passed[1], returned[0]), across, inner))
        far = [jnp.where(is_inner, a, b) for a, b in zip(returned, passed)]
        far = pack(where, half // 2, *shared(far))
        own[1] = after(own[1], passed[1], near)
    else:
        panels = [panel]
        for bit in range(low_bits, all_bits):
            panels = panels + [swapped(p, 1 << bit) for p in panels]
        others = [swapped(p, 1) for p in panels]
        near = pack(where, 0, panels, others)
        far = pack(where, half // 2, panels, others)
    from_xz = [swapped(after(from_z[0], from_x), 2)]
    from_z.append(swapped(own[1], 4))
    last = jnp.concatenate([from_x[cuts[2] :], own[2]])
    last = swapped(after(last, from_z[1], from_xz[0]), 4)
    from_xz.append(swapped(after(from_z[1], from_xz[0]), 2))

    squared = None
    sums = jnp.zeros((8, PC * width), jnp.float32)
    for n, (lo, hi) in enumerate(parts):
        if n < 2:
            received = [(from_z[n], 0), (from_xz[n], 0)]
        else:
            received = [(last, hi - lo), (last, 0)]
        mine, other = expand(
            [(tile_values, lo), (from_x, lo)] + received, order, index[lo:hi], near, far
        )
        got = swapped(other, 1)
        squared, sums = square(keep_tiles[lo:hi], sums, mine, got, lo, block_rows, squared)
    for bit in range(low_bits, all_bits - 1):
        sums = sums + swapped(sums, 1 << bit)
    got = swapped(sums, 1 << (all_bits - 1))
    return scale(float(CB * GC * width), sums, got, squared)


def solution(mesh):
    return jax.shard_map(
        shards,
        mesh=mesh,
        in_specs=(
            P(("groups", "grid"), None, None, None),
            P("groups", None, None),
            P(("groups", "grid"), None),
        ),
        out_specs=P(("groups", "grid"), None, None, None),
        check_vma=False,
    )
```

```python
import functools
import math

import jax
import jax.numpy as jnp
from jax import lax
from jax.experimental import pallas as pl
from jax.experimental.pallas import tpu as pltpu
from jax.sharding import PartitionSpec as P

GC = 8
CB = 12
PC = CB // 4
STRIPS = GC // 2
MIB = 1 << 20
SHORT = pl.CostEstimate(flops=0, bytes_accessed=1024, transcendentals=0)


def swapped(array, mask, among=lambda i: True):
    pairs = [(i, i ^ mask) for i in range(lax.axis_size("grid")) if among(i)]
    return lax.ppermute(array, "grid", pairs)


def inner(i):
    return (i ^ i >> 1) & (GC // 2) != 0


def outer(i):
    return not inner(i)


def panel_kernel(slot_ref, tiles_ref, *panel_refs):
    rows, _, width, _ = tiles_ref.shape
    first = pl.program_id(0) * rows
    steps = pl.num_programs(0) // len(panel_refs)

    for n, panel_ref in enumerate(panel_refs):

        @pl.when(pl.program_id(0) // steps == n)
        def _():
            @pl.loop(0, rows)
            def _(r):
                for p in range(PC):
                    slot = slot_ref[(first + r) * PC + p]
                    tile = tiles_ref[r, jnp.maximum(slot, 0)]
                    panel_ref[r, :, p * width : (p + 1) * width] = jnp.where(
                        slot >= 0, tile, jnp.zeros_like(tile)
                    )


def make_panel(tile_values, slots, parts):
    block_rows, slots_per_row, width, _ = tile_values.shape
    part_rows = block_rows // parts
    step = math.gcd(part_rows, 12)
    steps = part_rows // step

    def part_block(n):
        return pl.BlockSpec(
            (step, width, PC * width), lambda i, s: (jnp.clip(i - n * steps, 0, steps - 1), 0, 0)
        )

    return pl.pallas_call(
        panel_kernel,
        grid_spec=pltpu.PrefetchScalarGridSpec(
            num_scalar_prefetch=1,
            grid=(block_rows // step,),
            in_specs=[pl.BlockSpec((step, slots_per_row, width, width), lambda i, s: (i, 0, 0, 0))],
            out_specs=[part_block(n) for n in range(parts)],
        ),
        out_shape=[jax.ShapeDtypeStruct((part_rows, width, PC * width), jnp.bfloat16)] * parts,
        compiler_params=pltpu.CompilerParams(vmem_limit_bytes=12 * MIB),
        cost_estimate=SHORT,
        name="panel",
    )(slots.reshape(-1), tile_values)


def pack_kernel(first, parts, where_ref, *refs):
    sources, packed_ref, sem = refs[: 2 * parts], refs[-2], refs[-1]
    part_rows, _, half = sources[0].shape
    unit = math.gcd(CB, part_rows)
    for n in range(packed_ref.shape[0] // unit):
        part = where_ref[2 * (first + n)]
        offset = where_ref[2 * (first + n) + 1]
        for m in range(parts):

            @pl.when((part == m) | (parts == 1))
            def _():
                for side in range(2):
                    pltpu.make_async_copy(
                        sources[side * parts + m].at[pl.ds(offset, unit)],
                        packed_ref.at[pl.ds(n * unit, unit), :, pl.ds(side * half, half)],
                        sem.at[side],
                    ).start()
    for side in range(2):
        cols = pl.ds(side * half, half)
        pltpu.make_async_copy(
            packed_ref.at[:, :, cols], packed_ref.at[:, :, cols], sem.at[side]
        ).wait()


def pack(where, first, mine, others):
    parts = len(mine)
    _, width, half = mine[0].shape
    return pl.pallas_call(
        functools.partial(pack_kernel, first, parts),
        out_shape=jax.ShapeDtypeStruct((STRIPS // 2 * CB, width, 2 * half), jnp.bfloat16),
        in_specs=[pl.BlockSpec(memory_space=pltpu.SMEM)]
        + [pl.BlockSpec(memory_space=pl.ANY)] * (2 * parts),
        out_specs=pl.BlockSpec(memory_space=pltpu.VMEM),
        scratch_shapes=[pltpu.SemaphoreType.DMA((2,))],
        compiler_params=pltpu.CompilerParams(vmem_limit_bytes=8 * MIB),
        cost_estimate=SHORT,
        name="pack",
    )(where, *mine, *others)


def expand_kernel(first, plan, order_ref, index_ref, near_ref, far_ref, *refs):
    steps = len(plan)
    outs, (tiles, sums, tile_sem, sum_sem) = refs[-5 - steps : -4], refs[-4:]
    mine_ref, other_refs = outs[0], outs[1:]
    _, _, rows, slots, width, _ = tiles.shape
    half = PC * width
    total_rows = steps * rows

    def fetch(k):
        return [
            pltpu.make_async_copy(
                refs[source].at[pl.ds(offset, rows)], tiles.at[k % 2, q], tile_sem.at[k % 2, q]
            )
            for q, (source, offset) in enumerate(plan[k])
        ]

    def stores(k, r, slot):
        targets = (mine_ref.at[k * rows + r], other_refs[k].at[r])
        return [
            pltpu.make_async_copy(
                sums.at[slot, :, pl.ds(side * half, half)], target, sum_sem.at[slot, side]
            )
            for side, target in enumerate(targets)
        ]

    for copy in fetch(0):
        copy.start()
    for k in range(steps):
        if k + 1 < steps:
            for copy in fetch(k + 1):
                copy.start()
        for copy in fetch(k):
            copy.wait()

        @pl.loop(0, rows)
        def _(r):
            row = k * rows + r
            slot = lax.rem(row, 2)

            @pl.when(row >= 2)
            def _():
                for copy in stores(k, r, slot):
                    copy.wait()

            total = None
            for n in range(STRIPS):
                panel = near_ref if n < STRIPS // 2 else far_ref
                q = order_ref[n]
                for t in range(0, slots, 2):
                    base = (first + row) * (STRIPS * slots) + n * slots + t
                    left = jnp.concatenate(
                        [tiles[k % 2, q, r, t], tiles[k % 2, q, r, t + 1]], axis=1
                    )
                    right = jnp.concatenate(
                        [panel[index_ref[base]], panel[index_ref[base + 1]]], axis=0
                    )
                    term = jnp.dot(left, right, preferred_element_type=jnp.float32)
                    total = term if total is None else total + term
            sums[slot] = total
            for copy in stores(k, r, slot):
                copy.start()

    for row in range(max(total_rows - 2, 0), total_rows):
        for copy in stores(row // rows, row % rows, row % 2):
            copy.wait()


def expand(rows, first, pieces, order, index, near, far):
    arrays = []
    plan = []
    for piece in pieces:
        for array, _ in piece:
            if all(array is not a for a in arrays):
                arrays.append(array)
        plan.append([([array is a for a in arrays].index(True), row) for array, row in piece])
    _, slots, width, _ = arrays[0].shape
    half = PC * width
    anywhere = pl.BlockSpec(memory_space=pl.ANY)
    smem = pl.BlockSpec(memory_space=pltpu.SMEM)
    vmem = pl.BlockSpec(memory_space=pltpu.VMEM)
    out = pl.pallas_call(
        functools.partial(expand_kernel, first, plan),
        out_shape=[jax.ShapeDtypeStruct((len(plan) * rows, width, half), jnp.float32)]
        + [jax.ShapeDtypeStruct((rows, width, half), jnp.float32)] * len(plan),
        in_specs=[smem, smem, vmem, vmem] + [anywhere] * len(arrays),
        out_specs=[anywhere] * (1 + len(plan)),
        scratch_shapes=[
            pltpu.VMEM((2, STRIPS, rows, slots, width, width), jnp.bfloat16),
            pltpu.VMEM((2, width, 2 * half), jnp.float32),
            pltpu.SemaphoreType.DMA((2, STRIPS)),
            pltpu.SemaphoreType.DMA((2, 2)),
        ],
        compiler_params=pltpu.CompilerParams(vmem_limit_bytes=12 * MIB),
        cost_estimate=SHORT,
        name="expand",
    )(order, index, near, far, *arrays)
    return out[0], out[1:]


def square_kernel(lo, pieces, keep_ref, before_ref, mine_ref, *refs):
    got_refs, (squared_ref, sums_ref) = refs[:pieces], refs[-2:]
    rows, width, _ = mine_ref.shape
    first = lo + pl.program_id(0) * rows

    @pl.when(pl.program_id(0) == 0)
    def _():
        sums_ref[...] = before_ref[...]

    for n, got_ref in enumerate(got_refs):

        @pl.when(pl.program_id(0) == n)
        def _():
            @pl.loop(0, rows)
            def _(r):
                for p in range(PC):
                    keep = keep_ref[(first + r) * PC + p].astype(jnp.float32)
                    cols = slice(p * width, (p + 1) * width)
                    value = mine_ref[r, :, cols] + got_ref[r, :, cols]
                    value = value * value * keep
                    squared_ref[r, :, cols] = value
                    sums_ref[:, cols] += jnp.sum(value.reshape(width // 8, 8, width), axis=0)


def square(keep, before, mine, got, lo, total_rows, buffer):
    _, width, half = mine.shape
    step = got[0].shape[0]
    block = pl.BlockSpec((step, width, half), lambda i, s: (i, 0, 0))
    whole = pl.BlockSpec((step, width, half), lambda i, s: (0, 0, 0))
    target = pl.BlockSpec((step, width, half), lambda i, s: (lo // step + i, 0, 0))
    sums = pl.BlockSpec((8, half), lambda i, s: (0, 0))
    operands = [keep, before, mine, *got]
    in_specs = [sums, block] + [whole] * len(got)
    aliases = {}
    if buffer is not None:
        operands.append(buffer)
        in_specs.append(pl.BlockSpec(memory_space=pl.ANY))
        aliases = {len(operands) - 1: 0}
    return pl.pallas_call(
        functools.partial(square_kernel, lo, len(got)),
        grid_spec=pltpu.PrefetchScalarGridSpec(
            num_scalar_prefetch=1,
            grid=(len(got),),
            in_specs=in_specs,
            out_specs=(target, sums),
        ),
        out_shape=(
            jax.ShapeDtypeStruct((total_rows, width, half), jnp.float32),
            jax.ShapeDtypeStruct((8, half), jnp.float32),
        ),
        input_output_aliases=aliases,
        compiler_params=pltpu.CompilerParams(vmem_limit_bytes=16 * MIB),
        cost_estimate=SHORT,
        name="square",
    )(*operands)


def scale_kernel(count, sums_ref, got_ref, squared_ref, out_ref):
    step, width, _ = squared_ref.shape
    for p in range(PC):
        cols = slice(p * width, (p + 1) * width)
        sums = jnp.sum(sums_ref[:, cols] + got_ref[:, cols], axis=0, keepdims=True)
        inverse = 1.0 / (sums / count + 1e-6)
        for r in range(step):
            out_ref[r, p] = squared_ref[r, :, cols] * inverse


def scale(count, sums, got, squared):
    rows, width, half = squared.shape
    step = math.gcd(rows, 6)
    return pl.pallas_call(
        functools.partial(scale_kernel, count),
        grid=(rows // step,),
        in_specs=[pl.BlockSpec((8, half), lambda i: (0, 0))] * 2
        + [pl.BlockSpec((step, width, half), lambda i: (i, 0, 0))],
        out_specs=pl.BlockSpec((step, PC, width, width), lambda i: (i, 0, 0, 0)),
        out_shape=jax.ShapeDtypeStruct((rows, PC, width, width), jnp.float32),
        compiler_params=pltpu.CompilerParams(vmem_limit_bytes=12 * MIB),
        cost_estimate=SHORT,
        name="scale",
    )(sums, got, squared)


def after(array, *earlier):
    return lax.optimization_barrier((array, *earlier))[0]


def shards(tile_values, tile_columns, keep_tiles):
    devices = lax.axis_size("grid")
    device = lax.axis_index("grid")
    all_bits = devices.bit_length() - 1
    low_bits = GC.bit_length() - 1
    grid_rows = devices // GC
    row_strip = device // GC
    col_strip = device % GC
    block_rows, slots, width, _ = tile_values.shape
    pair = STRIPS // 2

    strip_rows = lax.dynamic_slice_in_dim(tile_columns, row_strip * block_rows, block_rows, 0)
    far_first = 0
    if block_rows == pair * 2 * CB:
        far_first = pair * (col_strip // (pair * 2) != row_strip).astype(jnp.int32)
    order = jnp.bitwise_xor(jnp.arange(STRIPS, dtype=jnp.int32), far_first)
    strips = jnp.bitwise_xor(col_strip, 2 * order)
    own = jnp.take(strip_rows, col_strip, axis=1)
    match = own[:, :, None] == jnp.arange(PC, dtype=jnp.int32)
    slot = jnp.max(
        jnp.where(match, jnp.arange(slots, dtype=jnp.int32)[None, :, None], -1), axis=1
    )
    index = jnp.take(strip_rows, strips, axis=1)
    index = index + CB * (jnp.arange(STRIPS, dtype=jnp.int32) % pair)[None, :, None]
    index = index.reshape(-1)
    keep = keep_tiles.reshape(-1)
    relayed = grid_rows == 2 and block_rows == 2 * pair * CB
    unit = math.gcd(CB, block_rows)
    unit_rows = strips[:, None] * CB + unit * jnp.arange(CB // unit, dtype=jnp.int32)
    part = jnp.bitwise_xor(unit_rows // block_rows, row_strip)
    offset = unit_rows % block_rows
    if relayed:
        part, offset = offset // (2 * CB), offset % CB
    where = jnp.stack([part, offset], axis=-1).reshape(-1)
    half = len(where) // 2

    def shared(pieces):
        odd = col_strip % 2 == 1
        pieces = [p[r : r + CB] for p in pieces for r in range(0, p.shape[0], CB)]
        kept = [jnp.where(odd, b, a) for a, b in zip(pieces[::2], pieces[1::2])]
        given = [jnp.where(odd, a, b) for a, b in zip(pieces[::2], pieces[1::2])]
        return kept, [swapped(p, 1) for p in given]

    rows = math.gcd(block_rows // 8, 6) if block_rows >= 8 else 1
    one, two = 3 * block_rows // 8, 2 * (3 * block_rows // 8)
    few = one // 3 if one >= 3 else one
    from_x = swapped(tile_values, 2)
    own = tile_values[:one]
    from_z = [swapped(own, 4)]
    panel = make_panel(after(tile_values, own), slot, 2 if relayed else 1)
    if relayed:
        across = GC + GC // 2
        near = pack(where, 0, *shared(panel))
        crossed = [swapped(panel[0], across, inner)]
        crossed.append(swapped(after(panel[1], crossed[0]), across, inner))
        inward, outward = [], []
        for got, piece in zip(crossed, panel):
            ready = from_z + inward + outward
            inward.append(swapped(after(piece, *ready), 4, outer))
            outward.append(swapped(after(got, *ready), 4, inner))
        returned = [swapped(after(inward[0], crossed[1]), across, inner)]
        returned.append(swapped(after(inward[1], returned[0]), across, inner))
        is_inner = inner(device)
        far = [jnp.where(is_inner, a, b) for a, b in zip(returned, outward)]
        far = pack(where, half // 2, *shared(far))
        tied = inward[1], outward[1], near
    else:
        panels = list(panel)
        for bit in range(low_bits, all_bits):
            panels = panels + [swapped(p, 1 << bit) for p in panels]
        others = [swapped(p, 1) for p in panels]
        near = pack(where, 0, panels, others)
        far = pack(where, half // 2, panels, others)
        tied = (near,)
    from_xz = [swapped(after(from_z[0][:few], from_x), 2)]
    if few < one:
        from_xz.append(swapped(after(from_z[0][few:], from_xz[0]), 2))
    later = after(tile_values, *tied, from_xz[0])
    from_z.append(swapped(later[one:two], 4))
    last = jnp.concatenate([from_x[two:], later[two:]])
    last = swapped(after(last, from_z[1], from_xz[-1]), 4)
    from_xz.append(swapped(after(from_z[1], from_xz[-1]), 2))

    def tiles_at(row):
        if row >= two:
            far_tiles = [(last, row - two + block_rows - two), (last, row - two)]
        elif row >= one:
            far_tiles = [(from_z[1], row - one), (from_xz[-1], row - one)]
        else:
            first = row < few
            far_tiles = [(from_z[0], row), (from_xz[0 if first else 1], row if first else row - few)]
        return [(tile_values, row), (from_x, row)] + far_tiles

    squared = None
    totals = []
    sums = jnp.zeros((8, PC * width), jnp.float32)
    for lo, hi in ((0, one), (one, two), (two, block_rows)):
        table = after(index, totals[0], got[0]) if len(totals) == 2 else index
        pieces = [tiles_at(row) for row in range(lo, hi, rows)]
        mine, other = expand(rows, lo, pieces, order, table, near, far)
        got = [swapped(a, 1) for a in other]
        squared, sums = square(keep, sums, mine, got, lo, block_rows, squared)
        totals.append(sums)
    for bit in range(low_bits, all_bits - 1):
        sums = sums + swapped(sums, 1 << bit)
    got = swapped(sums, 1 << (all_bits - 1))
    return scale(float(CB * GC * width), sums, got, squared)


def solution(mesh):
    return jax.shard_map(
        shards,
        mesh=mesh,
        in_specs=(
            P(("groups", "grid"), None, None, None),
            P("groups", None, None),
            P(("groups", "grid"), None),
        ),
        out_specs=P(("groups", "grid"), None, None, None),
        check_vma=False,
    )
```

```python
import functools
import math

import jax
import jax.numpy as jnp
from jax import lax
from jax.experimental import pallas as pl
from jax.experimental.pallas import tpu as pltpu
from jax.sharding import PartitionSpec as P

GC = 8
CB = 12
PC = CB // 4
STRIPS = GC // 2
MIB = 1 << 20
SHORT = pl.CostEstimate(flops=0, bytes_accessed=1024, transcendentals=0)


def swapped(array, mask, among=lambda i: True):
    pairs = [(i, i ^ mask) for i in range(lax.axis_size("grid")) if among(i)]
    return lax.ppermute(array, "grid", pairs)


def inner(i):
    return (i ^ i >> 1) & (GC // 2) != 0


def outer(i):
    return not inner(i)


def panel_kernel(first_steps, slot_ref, tiles_ref, first_ref, *panel_refs):
    rows, _, width, _ = tiles_ref.shape
    first = pl.program_id(0) * rows
    steps = pl.num_programs(0) // len(panel_refs)

    @pl.when(pl.program_id(0) < first_steps)
    def _():
        first_ref[...] = tiles_ref[...]

    for n, panel_ref in enumerate(panel_refs):

        @pl.when(pl.program_id(0) // steps == n)
        def _():
            @pl.loop(0, rows)
            def _(r):
                for p in range(PC):
                    slot = slot_ref[(first + r) * PC + p]
                    tile = tiles_ref[r, jnp.maximum(slot, 0)]
                    panel_ref[r, :, p * width : (p + 1) * width] = jnp.where(
                        slot >= 0, tile, jnp.zeros_like(tile)
                    )


def make_panel(tile_values, slots, parts, first_rows):
    block_rows, slots_per_row, width, _ = tile_values.shape
    part_rows = block_rows // parts
    step = math.gcd(math.gcd(part_rows, first_rows), 12)
    steps = part_rows // step
    first_steps = first_rows // step

    def part_block(n):
        return pl.BlockSpec(
            (step, width, PC * width), lambda i, s: (jnp.clip(i - n * steps, 0, steps - 1), 0, 0)
        )

    tile_shape = (slots_per_row, width, width)
    return pl.pallas_call(
        functools.partial(panel_kernel, first_steps),
        grid_spec=pltpu.PrefetchScalarGridSpec(
            num_scalar_prefetch=1,
            grid=(block_rows // step,),
            in_specs=[pl.BlockSpec((step, slots_per_row, width, width), lambda i, s: (i, 0, 0, 0))],
            out_specs=[
                pl.BlockSpec(
                    (step, *tile_shape), lambda i, s: (jnp.minimum(i, first_steps - 1), 0, 0, 0)
                )
            ]
            + [part_block(n) for n in range(parts)],
        ),
        out_shape=[jax.ShapeDtypeStruct((first_rows, *tile_shape), jnp.bfloat16)]
        + [jax.ShapeDtypeStruct((part_rows, width, PC * width), jnp.bfloat16)] * parts,
        compiler_params=pltpu.CompilerParams(vmem_limit_bytes=12 * MIB),
        cost_estimate=SHORT,
        name="panel",
    )(slots.reshape(-1), tile_values)


def pack_kernel(first, parts, where_ref, *refs):
    sources, packed_ref, sem = refs[: 2 * parts], refs[-2], refs[-1]
    part_rows, _, half = sources[0].shape
    unit = math.gcd(CB, part_rows)
    for n in range(packed_ref.shape[0] // unit):
        part = where_ref[2 * (first + n)]
        offset = where_ref[2 * (first + n) + 1]
        for m in range(parts):

            @pl.when((part == m) | (parts == 1))
            def _():
                for side in range(2):
                    pltpu.make_async_copy(
                        sources[side * parts + m].at[pl.ds(offset, unit)],
                        packed_ref.at[pl.ds(n * unit, unit), :, pl.ds(side * half, half)],
                        sem.at[side],
                    ).start()
    for side in range(2):
        cols = pl.ds(side * half, half)
        pltpu.make_async_copy(
            packed_ref.at[:, :, cols], packed_ref.at[:, :, cols], sem.at[side]
        ).wait()


def pack(where, first, mine, others):
    parts = len(mine)
    _, width, half = mine[0].shape
    return pl.pallas_call(
        functools.partial(pack_kernel, first, parts),
        out_shape=jax.ShapeDtypeStruct((STRIPS // 2 * CB, width, 2 * half), jnp.bfloat16),
        in_specs=[pl.BlockSpec(memory_space=pltpu.SMEM)]
        + [pl.BlockSpec(memory_space=pl.ANY)] * (2 * parts),
        out_specs=pl.BlockSpec(memory_space=pltpu.VMEM),
        scratch_shapes=[pltpu.SemaphoreType.DMA((2,))],
        compiler_params=pltpu.CompilerParams(vmem_limit_bytes=8 * MIB),
        cost_estimate=SHORT,
        name="pack",
    )(where, *mine, *others)


def expand_kernel(first, plan, order_ref, index_ref, near_ref, far_ref, *refs):
    steps = len(plan)
    outs, (tiles, sums, tile_sem, sum_sem) = refs[-5 - steps : -4], refs[-4:]
    mine_ref, other_refs = outs[0], outs[1:]
    _, _, rows, slots, width, _ = tiles.shape
    half = PC * width
    total_rows = steps * rows

    def fetch(k):
        return [
            pltpu.make_async_copy(
                refs[source].at[pl.ds(offset, rows)], tiles.at[k % 2, q], tile_sem.at[k % 2, q]
            )
            for q, (source, offset) in enumerate(plan[k])
        ]

    def stores(k, r, slot):
        targets = (mine_ref.at[k * rows + r], other_refs[k].at[r])
        return [
            pltpu.make_async_copy(
                sums.at[slot, :, pl.ds(side * half, half)], target, sum_sem.at[slot, side]
            )
            for side, target in enumerate(targets)
        ]

    for copy in fetch(0):
        copy.start()
    for k in range(steps):
        if k + 1 < steps:
            for copy in fetch(k + 1):
                copy.start()
        for copy in fetch(k):
            copy.wait()

        @pl.loop(0, rows)
        def _(r):
            row = k * rows + r
            slot = lax.rem(row, 2)

            @pl.when(row >= 2)
            def _():
                for copy in stores(k, r, slot):
                    copy.wait()

            total = None
            for n in range(STRIPS):
                panel = near_ref if n < STRIPS // 2 else far_ref
                q = order_ref[n]
                for t in range(0, slots, 2):
                    base = (first + row) * (STRIPS * slots) + n * slots + t
                    left = jnp.concatenate(
                        [tiles[k % 2, q, r, t], tiles[k % 2, q, r, t + 1]], axis=1
                    )
                    right = jnp.concatenate(
                        [panel[index_ref[base]], panel[index_ref[base + 1]]], axis=0
                    )
                    term = jnp.dot(left, right, preferred_element_type=jnp.float32)
                    total = term if total is None else total + term
            sums[slot] = total
            for copy in stores(k, r, slot):
                copy.start()

    for row in range(max(total_rows - 2, 0), total_rows):
        for copy in stores(row // rows, row % rows, row % 2):
            copy.wait()


def expand(rows, first, pieces, order, index, near, far):
    arrays = []
    plan = []
    for piece in pieces:
        for array, _ in piece:
            if all(array is not a for a in arrays):
                arrays.append(array)
        plan.append([([array is a for a in arrays].index(True), row) for array, row in piece])
    _, slots, width, _ = arrays[0].shape
    half = PC * width
    anywhere = pl.BlockSpec(memory_space=pl.ANY)
    smem = pl.BlockSpec(memory_space=pltpu.SMEM)
    vmem = pl.BlockSpec(memory_space=pltpu.VMEM)
    out = pl.pallas_call(
        functools.partial(expand_kernel, first, plan),
        out_shape=[jax.ShapeDtypeStruct((len(plan) * rows, width, half), jnp.float32)]
        + [jax.ShapeDtypeStruct((rows, width, half), jnp.float32)] * len(plan),
        in_specs=[smem, smem, vmem, vmem] + [anywhere] * len(arrays),
        out_specs=[pl.BlockSpec(memory_space=pltpu.HBM)] * (1 + len(plan)),
        scratch_shapes=[
            pltpu.VMEM((2, STRIPS, rows, slots, width, width), jnp.bfloat16),
            pltpu.VMEM((2, width, 2 * half), jnp.float32),
            pltpu.SemaphoreType.DMA((2, STRIPS)),
            pltpu.SemaphoreType.DMA((2, 2)),
        ],
        compiler_params=pltpu.CompilerParams(vmem_limit_bytes=12 * MIB),
        cost_estimate=SHORT,
        name="expand",
    )(order, index, near, far, *arrays)
    return out[0], out[1:]


def square_kernel(lo, pieces, keep_ref, before_ref, mine_ref, *refs):
    got_refs, (squared_ref, sums_ref) = refs[:pieces], refs[-2:]
    rows, width, _ = mine_ref.shape
    first = lo + pl.program_id(0) * rows

    @pl.when(pl.program_id(0) == 0)
    def _():
        sums_ref[...] = before_ref[...]

    for n, got_ref in enumerate(got_refs):

        @pl.when(pl.program_id(0) == n)
        def _():
            @pl.loop(0, rows)
            def _(r):
                for p in range(PC):
                    keep = keep_ref[(first + r) * PC + p].astype(jnp.float32)
                    cols = slice(p * width, (p + 1) * width)
                    value = mine_ref[r, :, cols] + got_ref[r, :, cols]
                    value = value * value * keep
                    squared_ref[r, :, cols] = value
                    sums_ref[:, cols] += jnp.sum(value.reshape(width // 8, 8, width), axis=0)


def square(keep, before, mine, got, lo, total_rows, buffer):
    _, width, half = mine.shape
    step = got[0].shape[0]
    block = pl.BlockSpec((step, width, half), lambda i, s: (i, 0, 0))
    whole = pl.BlockSpec((step, width, half), lambda i, s: (0, 0, 0))
    target = pl.BlockSpec((step, width, half), lambda i, s: (lo // step + i, 0, 0))
    sums = pl.BlockSpec((8, half), lambda i, s: (0, 0))
    operands = [keep, before, mine, *got]
    in_specs = [sums, block] + [whole] * len(got)
    aliases = {}
    if buffer is not None:
        operands.append(buffer)
        in_specs.append(pl.BlockSpec(memory_space=pl.ANY))
        aliases = {len(operands) - 1: 0}
    return pl.pallas_call(
        functools.partial(square_kernel, lo, len(got)),
        grid_spec=pltpu.PrefetchScalarGridSpec(
            num_scalar_prefetch=1,
            grid=(len(got),),
            in_specs=in_specs,
            out_specs=(target, sums),
        ),
        out_shape=(
            jax.ShapeDtypeStruct((total_rows, width, half), jnp.float32),
            jax.ShapeDtypeStruct((8, half), jnp.float32),
        ),
        input_output_aliases=aliases,
        compiler_params=pltpu.CompilerParams(vmem_limit_bytes=20 * MIB),
        cost_estimate=SHORT,
        name="square",
    )(*operands)


def scale_kernel(count, sums_ref, got_ref, squared_ref, out_ref):
    step, width, _ = squared_ref.shape
    for p in range(PC):
        cols = slice(p * width, (p + 1) * width)
        sums = jnp.sum(sums_ref[:, cols] + got_ref[:, cols], axis=0, keepdims=True)
        inverse = 1.0 / (sums / count + 1e-6)
        for r in range(step):
            out_ref[r, p] = squared_ref[r, :, cols] * inverse


def scale(count, sums, got, squared):
    rows, width, half = squared.shape
    step = math.gcd(rows, 6)
    return pl.pallas_call(
        functools.partial(scale_kernel, count),
        grid=(rows // step,),
        in_specs=[pl.BlockSpec((8, half), lambda i: (0, 0))] * 2
        + [pl.BlockSpec((step, width, half), lambda i: (i, 0, 0))],
        out_specs=pl.BlockSpec((step, PC, width, width), lambda i: (i, 0, 0, 0)),
        out_shape=jax.ShapeDtypeStruct((rows, PC, width, width), jnp.float32),
        compiler_params=pltpu.CompilerParams(vmem_limit_bytes=12 * MIB),
        cost_estimate=SHORT,
        name="scale",
    )(sums, got, squared)


def after(array, *earlier):
    return lax.optimization_barrier((array, *earlier))[0]


def shards(tile_values, tile_columns, keep_tiles):
    devices = lax.axis_size("grid")
    device = lax.axis_index("grid")
    all_bits = devices.bit_length() - 1
    low_bits = GC.bit_length() - 1
    grid_rows = devices // GC
    row_strip = device // GC
    col_strip = device % GC
    block_rows, slots, width, _ = tile_values.shape
    pair = STRIPS // 2

    strip_rows = lax.dynamic_slice_in_dim(tile_columns, row_strip * block_rows, block_rows, 0)
    far_first = 0
    if block_rows == pair * 2 * CB:
        far_first = pair * (col_strip // (pair * 2) != row_strip).astype(jnp.int32)
    order = jnp.bitwise_xor(jnp.arange(STRIPS, dtype=jnp.int32), far_first)
    strips = jnp.bitwise_xor(col_strip, 2 * order)
    own = jnp.take(strip_rows, col_strip, axis=1)
    match = own[:, :, None] == jnp.arange(PC, dtype=jnp.int32)
    slot = jnp.max(
        jnp.where(match, jnp.arange(slots, dtype=jnp.int32)[None, :, None], -1), axis=1
    )
    index = jnp.take(strip_rows, strips, axis=1)
    index = index + CB * (jnp.arange(STRIPS, dtype=jnp.int32) % pair)[None, :, None]
    index = index.reshape(-1)
    keep = keep_tiles.reshape(-1)
    relayed = grid_rows == 2 and block_rows == 2 * pair * CB
    unit = math.gcd(CB, block_rows)
    unit_rows = strips[:, None] * CB + unit * jnp.arange(CB // unit, dtype=jnp.int32)
    part = jnp.bitwise_xor(unit_rows // block_rows, row_strip)
    offset = unit_rows % block_rows
    if relayed:
        part, offset = offset // (2 * CB), offset % CB
    where = jnp.stack([part, offset], axis=-1).reshape(-1)
    half = len(where) // 2

    def shared(pieces):
        odd = col_strip % 2 == 1
        pieces = [p[r : r + CB] for p in pieces for r in range(0, p.shape[0], CB)]
        kept = [jnp.where(odd, b, a) for a, b in zip(pieces[::2], pieces[1::2])]
        given = [jnp.where(odd, a, b) for a, b in zip(pieces[::2], pieces[1::2])]
        return kept, [swapped(p, 1) for p in given]

    rows = block_rows // 16 or 1
    one, two = 8 * rows, 13 * rows
    if block_rows % 16:
        one, two = block_rows // 3, 2 * (block_rows // 3)
    few = one // 2 or one
    from_x = swapped(tile_values, 2)
    own, *panel = make_panel(tile_values, slot, 2 if relayed else 1, one)
    from_z = [swapped(own, 4)]
    if relayed:
        across = GC + GC // 2
        near = pack(where, 0, *shared(panel))
        crossed = [swapped(panel[0], across, inner)]
        crossed.append(swapped(after(panel[1], crossed[0]), across, inner))
        inward, outward = [], []
        for got, piece in zip(crossed, panel):
            ready = from_z + inward + outward
            inward.append(swapped(after(piece, *ready), 4, outer))
            outward.append(swapped(after(got, *ready), 4, inner))
        returned = [swapped(after(inward[0], crossed[1]), across, inner)]
        returned.append(swapped(after(inward[1], returned[0]), across, inner))
        is_inner = inner(device)
        far = [jnp.where(is_inner, a, b) for a, b in zip(returned, outward)]
        far = pack(where, half // 2, *shared(far))
        tied = inward[1], outward[1]
    else:
        panels = panel
        for bit in range(low_bits, all_bits):
            panels = panels + [swapped(p, 1 << bit) for p in panels]
        others = [swapped(p, 1) for p in panels]
        near = pack(where, 0, panels, others)
        far = pack(where, half // 2, panels, others)
        tied = ()
    from_xz = [swapped(after(from_z[0][:few], from_x), 2)]
    if few < one:
        from_xz.append(swapped(after(from_z[0][few:], from_xz[0]), 2))
    later = after(tile_values, near)
    from_z.append(swapped(after(later[one:two], *tied, from_xz[0]), 4))
    last = jnp.concatenate([from_x[two:], later[two:]])
    last = swapped(after(last, from_z[1], from_xz[-1]), 4)
    from_xz.append(swapped(after(from_z[1], from_xz[-1]), 2))

    def tiles_at(row):
        if row >= two:
            far_tiles = [(last, row - two + block_rows - two), (last, row - two)]
        elif row >= one:
            far_tiles = [(from_z[1], row - one), (from_xz[-1], row - one)]
        else:
            first = row < few
            far_tiles = [(from_z[0], row), (from_xz[0 if first else 1], row if first else row - few)]
        return [(tile_values, row), (from_x, row)] + far_tiles

    squared = None
    totals = []
    sums = jnp.zeros((8, PC * width), jnp.float32)
    for lo, hi in ((0, one), (one, two), (two, block_rows)):
        table = index
        if len(totals) == 2:
            table = after(index, totals[0], got[0])
        pieces = [tiles_at(row) for row in range(lo, hi, rows)]
        mine, other = expand(rows, lo, pieces, order, table, near, far)
        got = [swapped(a, 1) for a in other]
        squared, sums = square(keep, sums, mine, got, lo, block_rows, squared)
        totals.append(sums)
    for bit in range(low_bits, all_bits - 1):
        sums = sums + swapped(sums, 1 << bit)
    got = swapped(sums, 1 << (all_bits - 1))
    return scale(float(CB * GC * width), sums, got, squared)


def solution(mesh):
    return jax.shard_map(
        shards,
        mesh=mesh,
        in_specs=(
            P(("groups", "grid"), None, None, None),
            P("groups", None, None),
            P(("groups", "grid"), None),
        ),
        out_specs=P(("groups", "grid"), None, None, None),
        check_vma=False,
    )
```

```python
import functools
import math

import jax
import jax.numpy as jnp
from jax import lax
from jax.experimental import pallas as pl
from jax.experimental.pallas import tpu as pltpu
from jax.sharding import PartitionSpec as P

GC = 8
CB = 12
PC = CB // 4
STRIPS = GC // 2
MIB = 1 << 20
SHORT = pl.CostEstimate(flops=0, bytes_accessed=1024, transcendentals=0)


def swapped(array, mask, among=lambda i: True):
    pairs = [(i, i ^ mask) for i in range(lax.axis_size("grid")) if among(i)]
    return lax.ppermute(array, "grid", pairs)


def inner(i):
    return (i ^ i >> 1) & (GC // 2) != 0


def outer(i):
    return not inner(i)


def panel_kernel(first_steps, slot_ref, tiles_ref, first_ref, *panel_refs):
    rows, _, width, _ = tiles_ref.shape
    first = pl.program_id(0) * rows
    steps = pl.num_programs(0) // len(panel_refs)

    @pl.when(pl.program_id(0) < first_steps)
    def _():
        first_ref[...] = tiles_ref[...]

    for n, panel_ref in enumerate(panel_refs):

        @pl.when(pl.program_id(0) // steps == n)
        def _():
            @pl.loop(0, rows)
            def _(r):
                for p in range(PC):
                    slot = slot_ref[(first + r) * PC + p]
                    tile = tiles_ref[r, jnp.maximum(slot, 0)]
                    panel_ref[r, :, p * width : (p + 1) * width] = jnp.where(
                        slot >= 0, tile, jnp.zeros_like(tile)
                    )


def make_panel(tile_values, slots, parts, first_rows):
    block_rows, slots_per_row, width, _ = tile_values.shape
    part_rows = block_rows // parts
    step = math.gcd(math.gcd(part_rows, first_rows), 12)
    steps = part_rows // step
    first_steps = first_rows // step

    def part_block(n):
        return pl.BlockSpec(
            (step, width, PC * width), lambda i, s: (jnp.clip(i - n * steps, 0, steps - 1), 0, 0)
        )

    tile_shape = (slots_per_row, width, width)
    return pl.pallas_call(
        functools.partial(panel_kernel, first_steps),
        grid_spec=pltpu.PrefetchScalarGridSpec(
            num_scalar_prefetch=1,
            grid=(block_rows // step,),
            in_specs=[pl.BlockSpec((step, slots_per_row, width, width), lambda i, s: (i, 0, 0, 0))],
            out_specs=[
                pl.BlockSpec(
                    (step, *tile_shape), lambda i, s: (jnp.minimum(i, first_steps - 1), 0, 0, 0)
                )
            ]
            + [part_block(n) for n in range(parts)],
        ),
        out_shape=[jax.ShapeDtypeStruct((first_rows, *tile_shape), jnp.bfloat16)]
        + [jax.ShapeDtypeStruct((part_rows, width, PC * width), jnp.bfloat16)] * parts,
        compiler_params=pltpu.CompilerParams(vmem_limit_bytes=12 * MIB),
        cost_estimate=SHORT,
        name="panel",
    )(slots.reshape(-1), tile_values)


def pack_kernel(first, parts, where_ref, *refs):
    sources, packed_ref, sem = refs[: 2 * parts], refs[-2], refs[-1]
    part_rows, _, half = sources[0].shape
    unit = math.gcd(CB, part_rows)
    for n in range(packed_ref.shape[0] // unit):
        part = where_ref[2 * (first + n)]
        offset = where_ref[2 * (first + n) + 1]
        for m in range(parts):

            @pl.when((part == m) | (parts == 1))
            def _():
                for side in range(2):
                    pltpu.make_async_copy(
                        sources[side * parts + m].at[pl.ds(offset, unit)],
                        packed_ref.at[pl.ds(n * unit, unit), :, pl.ds(side * half, half)],
                        sem.at[side],
                    ).start()
    for side in range(2):
        cols = pl.ds(side * half, half)
        pltpu.make_async_copy(
            packed_ref.at[:, :, cols], packed_ref.at[:, :, cols], sem.at[side]
        ).wait()


def pack(where, first, mine, others):
    parts = len(mine)
    _, width, half = mine[0].shape
    return pl.pallas_call(
        functools.partial(pack_kernel, first, parts),
        out_shape=jax.ShapeDtypeStruct((STRIPS // 2 * CB, width, 2 * half), jnp.bfloat16),
        in_specs=[pl.BlockSpec(memory_space=pltpu.SMEM)]
        + [pl.BlockSpec(memory_space=pl.ANY)] * (2 * parts),
        out_specs=pl.BlockSpec(memory_space=pltpu.VMEM),
        scratch_shapes=[pltpu.SemaphoreType.DMA((2,))],
        compiler_params=pltpu.CompilerParams(vmem_limit_bytes=8 * MIB),
        cost_estimate=SHORT,
        name="pack",
    )(where, *mine, *others)


def expand_kernel(first, plan, order_ref, index_ref, near_ref, far_ref, *refs):
    steps = len(plan)
    outs, (tiles, sums, tile_sem, sum_sem) = refs[-5 - steps : -4], refs[-4:]
    mine_ref, other_refs = outs[0], outs[1:]
    _, _, rows, slots, width, _ = tiles.shape
    half = PC * width
    total_rows = steps * rows

    def fetch(k):
        return [
            pltpu.make_async_copy(
                refs[source].at[pl.ds(offset, rows)], tiles.at[k % 2, q], tile_sem.at[k % 2, q]
            )
            for q, (source, offset) in enumerate(plan[k])
        ]

    def stores(k, r, slot):
        targets = (mine_ref.at[k * rows + r], other_refs[k].at[r])
        return [
            pltpu.make_async_copy(
                sums.at[slot, :, pl.ds(side * half, half)], target, sum_sem.at[slot, side]
            )
            for side, target in enumerate(targets)
        ]

    for copy in fetch(0):
        copy.start()
    for k in range(steps):
        if k + 1 < steps:
            for copy in fetch(k + 1):
                copy.start()
        for copy in fetch(k):
            copy.wait()

        @pl.loop(0, rows)
        def _(r):
            row = k * rows + r
            slot = lax.rem(row, 2)

            @pl.when(row >= 2)
            def _():
                for copy in stores(k, r, slot):
                    copy.wait()

            total = None
            for n in range(STRIPS):
                panel = near_ref if n < STRIPS // 2 else far_ref
                q = order_ref[n]
                for t in range(0, slots, 2):
                    base = (first + row) * (STRIPS * slots) + n * slots + t
                    left = jnp.concatenate(
                        [tiles[k % 2, q, r, t], tiles[k % 2, q, r, t + 1]], axis=1
                    )
                    right = jnp.concatenate(
                        [panel[index_ref[base]], panel[index_ref[base + 1]]], axis=0
                    )
                    term = jnp.dot(left, right, preferred_element_type=jnp.float32)
                    total = term if total is None else total + term
            sums[slot] = total
            for copy in stores(k, r, slot):
                copy.start()

    for row in range(max(total_rows - 2, 0), total_rows):
        for copy in stores(row // rows, row % rows, row % 2):
            copy.wait()


def expand(rows, first, pieces, order, index, near, far):
    arrays = []
    plan = []
    for piece in pieces:
        for array, _ in piece:
            if all(array is not a for a in arrays):
                arrays.append(array)
        plan.append([([array is a for a in arrays].index(True), row) for array, row in piece])
    _, slots, width, _ = arrays[0].shape
    half = PC * width
    anywhere = pl.BlockSpec(memory_space=pl.ANY)
    smem = pl.BlockSpec(memory_space=pltpu.SMEM)
    vmem = pl.BlockSpec(memory_space=pltpu.VMEM)
    out = pl.pallas_call(
        functools.partial(expand_kernel, first, plan),
        out_shape=[jax.ShapeDtypeStruct((len(plan) * rows, width, half), jnp.float32)]
        + [jax.ShapeDtypeStruct((rows, width, half), jnp.float32)] * len(plan),
        in_specs=[smem, smem, vmem, vmem] + [anywhere] * len(arrays),
        out_specs=[pl.BlockSpec(memory_space=pltpu.HBM)] * (1 + len(plan)),
        scratch_shapes=[
            pltpu.VMEM((2, STRIPS, rows, slots, width, width), jnp.bfloat16),
            pltpu.VMEM((2, width, 2 * half), jnp.float32),
            pltpu.SemaphoreType.DMA((2, STRIPS)),
            pltpu.SemaphoreType.DMA((2, 2)),
        ],
        compiler_params=pltpu.CompilerParams(vmem_limit_bytes=12 * MIB),
        cost_estimate=SHORT,
        name="expand",
    )(order, index, near, far, *arrays)
    return out[0], out[1:]


def square_kernel(lo, pieces, keep_ref, before_ref, mine_ref, *refs):
    got_refs, (squared_ref, sums_ref) = refs[:pieces], refs[-2:]
    rows, width, _ = mine_ref.shape
    first = lo + pl.program_id(0) * rows

    @pl.when(pl.program_id(0) == 0)
    def _():
        sums_ref[...] = before_ref[...]

    for n, got_ref in enumerate(got_refs):

        @pl.when(pl.program_id(0) == n)
        def _():
            @pl.loop(0, rows)
            def _(r):
                for p in range(PC):
                    keep = keep_ref[(first + r) * PC + p].astype(jnp.float32)
                    cols = slice(p * width, (p + 1) * width)
                    value = mine_ref[r, :, cols] + got_ref[r, :, cols]
                    value = value * value * keep
                    squared_ref[r, :, cols] = value
                    sums_ref[:, cols] += jnp.sum(value.reshape(width // 8, 8, width), axis=0)


def square(keep, before, mine, got, lo, total_rows, buffer):
    _, width, half = mine.shape
    step = got[0].shape[0]
    block = pl.BlockSpec((step, width, half), lambda i, s: (i, 0, 0))
    whole = pl.BlockSpec((step, width, half), lambda i, s: (0, 0, 0))
    target = pl.BlockSpec((step, width, half), lambda i, s: (lo // step + i, 0, 0))
    sums = pl.BlockSpec((8, half), lambda i, s: (0, 0))
    operands = [keep, before, mine, *got]
    in_specs = [sums, block] + [whole] * len(got)
    aliases = {}
    if buffer is not None:
        operands.append(buffer)
        in_specs.append(pl.BlockSpec(memory_space=pl.ANY))
        aliases = {len(operands) - 1: 0}
    return pl.pallas_call(
        functools.partial(square_kernel, lo, len(got)),
        grid_spec=pltpu.PrefetchScalarGridSpec(
            num_scalar_prefetch=1,
            grid=(len(got),),
            in_specs=in_specs,
            out_specs=(target, sums),
        ),
        out_shape=(
            jax.ShapeDtypeStruct((total_rows, width, half), jnp.float32),
            jax.ShapeDtypeStruct((8, half), jnp.float32),
        ),
        input_output_aliases=aliases,
        compiler_params=pltpu.CompilerParams(vmem_limit_bytes=20 * MIB),
        cost_estimate=SHORT,
        name="square",
    )(*operands)


def scale_kernel(count, sums_ref, got_ref, squared_ref, out_ref):
    step, width, _ = squared_ref.shape
    for p in range(PC):
        cols = slice(p * width, (p + 1) * width)
        sums = jnp.sum(sums_ref[:, cols] + got_ref[:, cols], axis=0, keepdims=True)
        inverse = 1.0 / (sums / count + 1e-6)
        for r in range(step):
            out_ref[r, p] = squared_ref[r, :, cols] * inverse


def scale(count, sums, got, squared):
    rows, width, half = squared.shape
    step = math.gcd(rows, 6)
    return pl.pallas_call(
        functools.partial(scale_kernel, count),
        grid=(rows // step,),
        in_specs=[pl.BlockSpec((8, half), lambda i: (0, 0))] * 2
        + [pl.BlockSpec((step, width, half), lambda i: (i, 0, 0))],
        out_specs=pl.BlockSpec((step, PC, width, width), lambda i: (i, 0, 0, 0)),
        out_shape=jax.ShapeDtypeStruct((rows, PC, width, width), jnp.float32),
        compiler_params=pltpu.CompilerParams(vmem_limit_bytes=12 * MIB),
        cost_estimate=SHORT,
        name="scale",
    )(sums, got, squared)


def after(array, *earlier):
    return lax.optimization_barrier((array, *earlier))[0]


def shards(tile_values, tile_columns, keep_tiles):
    devices = lax.axis_size("grid")
    device = lax.axis_index("grid")
    all_bits = devices.bit_length() - 1
    low_bits = GC.bit_length() - 1
    grid_rows = devices // GC
    row_strip = device // GC
    col_strip = device % GC
    block_rows, slots, width, _ = tile_values.shape
    pair = STRIPS // 2

    strip_rows = lax.dynamic_slice_in_dim(tile_columns, row_strip * block_rows, block_rows, 0)
    far_first = 0
    if block_rows == pair * 2 * CB:
        far_first = pair * (col_strip // (pair * 2) != row_strip).astype(jnp.int32)
    order = jnp.bitwise_xor(jnp.arange(STRIPS, dtype=jnp.int32), far_first)
    strips = jnp.bitwise_xor(col_strip, 2 * order)
    own = jnp.take(strip_rows, col_strip, axis=1)
    match = own[:, :, None] == jnp.arange(PC, dtype=jnp.int32)
    slot = jnp.max(
        jnp.where(match, jnp.arange(slots, dtype=jnp.int32)[None, :, None], -1), axis=1
    )
    index = jnp.take(strip_rows, strips, axis=1)
    index = index + CB * (jnp.arange(STRIPS, dtype=jnp.int32) % pair)[None, :, None]
    index = index.reshape(-1)
    keep = keep_tiles.reshape(-1)
    relayed = grid_rows == 2 and block_rows == 2 * pair * CB
    unit = math.gcd(CB, block_rows)
    unit_rows = strips[:, None] * CB + unit * jnp.arange(CB // unit, dtype=jnp.int32)
    part = jnp.bitwise_xor(unit_rows // block_rows, row_strip)
    offset = unit_rows % block_rows
    if relayed:
        part, offset = offset // (2 * CB), offset % CB
    where = jnp.stack([part, offset], axis=-1).reshape(-1)
    half = len(where) // 2

    def shared(pieces):
        odd = col_strip % 2 == 1
        pieces = [p[r : r + CB] for p in pieces for r in range(0, p.shape[0], CB)]
        kept = [jnp.where(odd, b, a) for a, b in zip(pieces[::2], pieces[1::2])]
        given = [jnp.where(odd, a, b) for a, b in zip(pieces[::2], pieces[1::2])]
        return kept, [swapped(p, 1) for p in given]

    rows = block_rows // 16 or 1
    one, two = 8 * rows, 13 * rows
    if block_rows % 16:
        one, two = block_rows // 3, 2 * (block_rows // 3)
    few = one // 2 or one
    from_x = swapped(tile_values, 2)
    own, *panel = make_panel(tile_values, slot, 2 if relayed else 1, one)
    from_z = [swapped(own, 4)]
    if relayed:
        across = GC + GC // 2
        near = pack(where, 0, *shared(panel))
        crossed = [swapped(panel[0], across, inner)]
        crossed.append(swapped(after(panel[1], crossed[0]), across, inner))
        inward, outward = [], []
        for got, piece in zip(crossed, panel):
            ready = from_z + inward + outward
            inward.append(swapped(after(piece, *ready), 4, outer))
            outward.append(swapped(after(got, *ready), 4, inner))
        returned = [swapped(after(inward[0], crossed[1]), across, inner)]
        returned.append(swapped(after(inward[1], returned[0]), across, inner))
        is_inner = inner(device)
        kept, received = [], []
        for a, b in zip(returned, outward):
            k, r = shared([jnp.where(is_inner, a, b)])
            kept += k
            received += r
        far = pack(where, half // 2, kept, received)
        tied = [inward[1], outward[1]]
    else:
        panels = panel
        for bit in range(low_bits, all_bits):
            panels = panels + [swapped(p, 1 << bit) for p in panels]
        others = [swapped(p, 1) for p in panels]
        near = pack(where, 0, panels, others)
        far = pack(where, half // 2, panels, others)
        tied = []
    from_xz = [swapped(after(from_z[0][:few], from_x), 2)]
    if few < one:
        from_xz.append(swapped(after(from_z[0][few:], from_xz[0]), 2))
    later = after(tile_values, near)
    last = jnp.concatenate([from_x[two:], later[two:]])
    tied = tied + [from_xz[0], last, keep, index]
    from_z.append(swapped(after(later[one:two], *tied), 4))
    last = swapped(after(last, from_z[1], from_xz[-1]), 4)
    from_xz.append(swapped(after(from_z[1], from_xz[-1]), 2))

    def tiles_at(row):
        if row >= two:
            far_tiles = [(last, row - two + block_rows - two), (last, row - two)]
        elif row >= one:
            far_tiles = [(from_z[1], row - one), (from_xz[-1], row - one)]
        else:
            first = row < few
            far_tiles = [(from_z[0], row), (from_xz[0 if first else 1], row if first else row - few)]
        return [(tile_values, row), (from_x, row)] + far_tiles

    squared = None
    keep, index = lax.optimization_barrier((keep, index, from_z[1]))[:2]
    totals = []
    sums = jnp.zeros((8, PC * width), jnp.float32)
    for lo, hi in ((0, one), (one, two), (two, block_rows)):
        table = index
        if len(totals) == 2:
            table = after(index, totals[0], got[0])
        pieces = [tiles_at(row) for row in range(lo, hi, rows)]
        mine, other = expand(rows, lo, pieces, order, table, near, far)
        got = [swapped(a, 1) for a in other]
        squared, sums = square(keep, sums, mine, got, lo, block_rows, squared)
        totals.append(sums)
    for bit in range(low_bits, all_bits - 1):
        sums = sums + swapped(sums, 1 << bit)
    got = swapped(sums, 1 << (all_bits - 1))
    return scale(float(CB * GC * width), sums, got, squared)


def solution(mesh):
    return jax.shard_map(
        shards,
        mesh=mesh,
        in_specs=(
            P(("groups", "grid"), None, None, None),
            P("groups", None, None),
            P(("groups", "grid"), None),
        ),
        out_specs=P(("groups", "grid"), None, None, None),
        check_vma=False,
    )
```

```python
import functools
import math

import jax
import jax.numpy as jnp
from jax import lax
from jax.experimental import pallas as pl
from jax.experimental.pallas import tpu as pltpu
from jax.sharding import PartitionSpec as P

GC = 8
CB = 12
PC = CB // 4
STRIPS = GC // 2
MIB = 1 << 20
SHORT = pl.CostEstimate(flops=0, bytes_accessed=1024, transcendentals=0)


def swapped(array, mask, among=lambda i: True):
    pairs = [(i, i ^ mask) for i in range(lax.axis_size("grid")) if among(i)]
    return lax.ppermute(array, "grid", pairs)


def inner(i):
    return (i ^ i >> 1) & (GC // 2) != 0


def outer(i):
    return not inner(i)


def panel_kernel(first_steps, slot_ref, tiles_ref, first_ref, *panel_refs):
    rows, _, width, _ = tiles_ref.shape
    first = pl.program_id(0) * rows
    steps = pl.num_programs(0) // len(panel_refs)

    @pl.when(pl.program_id(0) < first_steps)
    def _():
        first_ref[...] = tiles_ref[...]

    for n, panel_ref in enumerate(panel_refs):

        @pl.when(pl.program_id(0) // steps == n)
        def _():
            @pl.loop(0, rows)
            def _(r):
                for p in range(PC):
                    slot = slot_ref[(first + r) * PC + p]
                    tile = tiles_ref[r, jnp.maximum(slot, 0)]
                    panel_ref[r, :, p * width : (p + 1) * width] = jnp.where(
                        slot >= 0, tile, jnp.zeros_like(tile)
                    )


def make_panel(tile_values, slots, parts, first_rows):
    block_rows, slots_per_row, width, _ = tile_values.shape
    part_rows = block_rows // parts
    step = math.gcd(math.gcd(part_rows, first_rows), 12)
    steps = part_rows // step
    first_steps = first_rows // step

    def part_block(n):
        return pl.BlockSpec(
            (step, width, PC * width), lambda i, s: (jnp.clip(i - n * steps, 0, steps - 1), 0, 0)
        )

    tile_shape = (slots_per_row, width, width)
    return pl.pallas_call(
        functools.partial(panel_kernel, first_steps),
        grid_spec=pltpu.PrefetchScalarGridSpec(
            num_scalar_prefetch=1,
            grid=(block_rows // step,),
            in_specs=[pl.BlockSpec((step, slots_per_row, width, width), lambda i, s: (i, 0, 0, 0))],
            out_specs=[
                pl.BlockSpec(
                    (step, *tile_shape), lambda i, s: (jnp.minimum(i, first_steps - 1), 0, 0, 0)
                )
            ]
            + [part_block(n) for n in range(parts)],
        ),
        out_shape=[jax.ShapeDtypeStruct((first_rows, *tile_shape), jnp.bfloat16)]
        + [jax.ShapeDtypeStruct((part_rows, width, PC * width), jnp.bfloat16)] * parts,
        compiler_params=pltpu.CompilerParams(vmem_limit_bytes=12 * MIB),
        cost_estimate=SHORT,
        name="panel",
    )(slots.reshape(-1), tile_values)


def pack_kernel(first, parts, where_ref, *refs):
    sources, packed_ref, sem = refs[: 2 * parts], refs[-2], refs[-1]
    part_rows, _, half = sources[0].shape
    unit = math.gcd(CB, part_rows)
    for n in range(packed_ref.shape[0] // unit):
        part = where_ref[2 * (first + n)]
        offset = where_ref[2 * (first + n) + 1]
        for m in range(parts):

            @pl.when((part == m) | (parts == 1))
            def _():
                for side in range(2):
                    pltpu.make_async_copy(
                        sources[side * parts + m].at[pl.ds(offset, unit)],
                        packed_ref.at[pl.ds(n * unit, unit), :, pl.ds(side * half, half)],
                        sem.at[side],
                    ).start()
    for side in range(2):
        cols = pl.ds(side * half, half)
        pltpu.make_async_copy(
            packed_ref.at[:, :, cols], packed_ref.at[:, :, cols], sem.at[side]
        ).wait()


def pack(where, first, mine, others):
    parts = len(mine)
    _, width, half = mine[0].shape
    return pl.pallas_call(
        functools.partial(pack_kernel, first, parts),
        out_shape=jax.ShapeDtypeStruct((STRIPS // 2 * CB, width, 2 * half), jnp.bfloat16),
        in_specs=[pl.BlockSpec(memory_space=pltpu.SMEM)]
        + [pl.BlockSpec(memory_space=pl.ANY)] * (2 * parts),
        out_specs=pl.BlockSpec(memory_space=pltpu.VMEM),
        scratch_shapes=[pltpu.SemaphoreType.DMA((2,))],
        compiler_params=pltpu.CompilerParams(vmem_limit_bytes=8 * MIB),
        cost_estimate=SHORT,
        name="pack",
    )(where, *mine, *others)


def expand_kernel(first, plan, order_ref, index_ref, near_ref, far_ref, *refs):
    steps = len(plan)
    outs, (tiles, sums, tile_sem, sum_sem) = refs[-5 - steps : -4], refs[-4:]
    mine_ref, other_refs = outs[0], outs[1:]
    _, _, rows, slots, width, _ = tiles.shape
    half = PC * width
    total_rows = steps * rows

    def fetch(k):
        return [
            pltpu.make_async_copy(
                refs[source].at[pl.ds(offset, rows)], tiles.at[k % 2, q], tile_sem.at[k % 2, q]
            )
            for q, (source, offset) in enumerate(plan[k])
        ]

    def stores(k, r, slot):
        targets = (mine_ref.at[k * rows + r], other_refs[k].at[r])
        return [
            pltpu.make_async_copy(
                sums.at[slot, :, pl.ds(side * half, half)], target, sum_sem.at[slot, side]
            )
            for side, target in enumerate(targets)
        ]

    for copy in fetch(0):
        copy.start()
    for k in range(steps):
        if k + 1 < steps:
            for copy in fetch(k + 1):
                copy.start()
        for copy in fetch(k):
            copy.wait()

        @pl.loop(0, rows)
        def _(r):
            row = k * rows + r
            slot = lax.rem(row, 2)

            @pl.when(row >= 2)
            def _():
                for copy in stores(k, r, slot):
                    copy.wait()

            total = None
            for n in range(STRIPS):
                panel = near_ref if n < STRIPS // 2 else far_ref
                q = order_ref[n]
                for t in range(0, slots, 2):
                    base = (first + row) * (STRIPS * slots) + n * slots + t
                    left = jnp.concatenate(
                        [tiles[k % 2, q, r, t], tiles[k % 2, q, r, t + 1]], axis=1
                    )
                    right = jnp.concatenate(
                        [panel[index_ref[base]], panel[index_ref[base + 1]]], axis=0
                    )
                    term = jnp.dot(left, right, preferred_element_type=jnp.float32)
                    total = term if total is None else total + term
            sums[slot] = total
            for copy in stores(k, r, slot):
                copy.start()

    for row in range(max(total_rows - 2, 0), total_rows):
        for copy in stores(row // rows, row % rows, row % 2):
            copy.wait()


def expand(rows, first, pieces, order, index, near, far):
    arrays = []
    plan = []
    for piece in pieces:
        for array, _ in piece:
            if all(array is not a for a in arrays):
                arrays.append(array)
        plan.append([([array is a for a in arrays].index(True), row) for array, row in piece])
    _, slots, width, _ = arrays[0].shape
    half = PC * width
    anywhere = pl.BlockSpec(memory_space=pl.ANY)
    smem = pl.BlockSpec(memory_space=pltpu.SMEM)
    vmem = pl.BlockSpec(memory_space=pltpu.VMEM)
    out = pl.pallas_call(
        functools.partial(expand_kernel, first, plan),
        out_shape=[jax.ShapeDtypeStruct((len(plan) * rows, width, half), jnp.float32)]
        + [jax.ShapeDtypeStruct((rows, width, half), jnp.float32)] * len(plan),
        in_specs=[smem, smem, vmem, vmem] + [anywhere] * len(arrays),
        out_specs=[pl.BlockSpec(memory_space=pltpu.HBM)] * (1 + len(plan)),
        scratch_shapes=[
            pltpu.VMEM((2, STRIPS, rows, slots, width, width), jnp.bfloat16),
            pltpu.VMEM((2, width, 2 * half), jnp.float32),
            pltpu.SemaphoreType.DMA((2, STRIPS)),
            pltpu.SemaphoreType.DMA((2, 2)),
        ],
        compiler_params=pltpu.CompilerParams(vmem_limit_bytes=12 * MIB),
        cost_estimate=SHORT,
        name="expand",
    )(order, index, near, far, *arrays)
    return out[0], out[1:]


def square_kernel(lo, pieces, keep_ref, before_ref, mine_ref, *refs):
    got_refs, (squared_ref, sums_ref) = refs[:pieces], refs[-2:]
    rows, width, _ = mine_ref.shape
    first = lo + pl.program_id(0) * rows

    @pl.when(pl.program_id(0) == 0)
    def _():
        sums_ref[...] = before_ref[...]

    for n, got_ref in enumerate(got_refs):

        @pl.when(pl.program_id(0) == n)
        def _():
            @pl.loop(0, rows)
            def _(r):
                for p in range(PC):
                    keep = keep_ref[(first + r) * PC + p].astype(jnp.float32)
                    cols = slice(p * width, (p + 1) * width)
                    value = mine_ref[r, :, cols] + got_ref[r, :, cols]
                    value = value * value * keep
                    squared_ref[r, :, cols] = value
                    sums_ref[:, cols] += jnp.sum(value.reshape(width // 8, 8, width), axis=0)


def square(keep, before, mine, got, lo, total_rows, buffer):
    _, width, half = mine.shape
    step = got[0].shape[0]
    block = pl.BlockSpec((step, width, half), lambda i, s: (i, 0, 0))
    whole = pl.BlockSpec((step, width, half), lambda i, s: (0, 0, 0))
    target = pl.BlockSpec((step, width, half), lambda i, s: (lo // step + i, 0, 0))
    sums = pl.BlockSpec((8, half), lambda i, s: (0, 0))
    operands = [keep, before, mine, *got]
    in_specs = [sums, block] + [whole] * len(got)
    aliases = {}
    if buffer is not None:
        operands.append(buffer)
        in_specs.append(pl.BlockSpec(memory_space=pl.ANY))
        aliases = {len(operands) - 1: 0}
    return pl.pallas_call(
        functools.partial(square_kernel, lo, len(got)),
        grid_spec=pltpu.PrefetchScalarGridSpec(
            num_scalar_prefetch=1,
            grid=(len(got),),
            in_specs=in_specs,
            out_specs=(target, sums),
        ),
        out_shape=(
            jax.ShapeDtypeStruct((total_rows, width, half), jnp.float32),
            jax.ShapeDtypeStruct((8, half), jnp.float32),
        ),
        input_output_aliases=aliases,
        compiler_params=pltpu.CompilerParams(vmem_limit_bytes=20 * MIB),
        cost_estimate=SHORT,
        name="square",
    )(*operands)


def scale_kernel(count, sums_ref, got_ref, squared_ref, out_ref):
    step, width, _ = squared_ref.shape
    for p in range(PC):
        cols = slice(p * width, (p + 1) * width)
        sums = jnp.sum(sums_ref[:, cols] + got_ref[:, cols], axis=0, keepdims=True)
        inverse = 1.0 / (sums / count + 1e-6)
        for r in range(step):
            out_ref[r, p] = squared_ref[r, :, cols] * inverse


def scale(count, sums, got, squared):
    rows, width, half = squared.shape
    step = math.gcd(rows, 6)
    return pl.pallas_call(
        functools.partial(scale_kernel, count),
        grid=(rows // step,),
        in_specs=[pl.BlockSpec((8, half), lambda i: (0, 0))] * 2
        + [pl.BlockSpec((step, width, half), lambda i: (i, 0, 0))],
        out_specs=pl.BlockSpec((step, PC, width, width), lambda i: (i, 0, 0, 0)),
        out_shape=jax.ShapeDtypeStruct((rows, PC, width, width), jnp.float32),
        compiler_params=pltpu.CompilerParams(vmem_limit_bytes=12 * MIB),
        cost_estimate=SHORT,
        name="scale",
    )(sums, got, squared)


def after(array, *earlier):
    return lax.optimization_barrier((array, *earlier))[0]


def shards(tile_values, tile_columns, keep_tiles):
    devices = lax.axis_size("grid")
    device = lax.axis_index("grid")
    all_bits = devices.bit_length() - 1
    low_bits = GC.bit_length() - 1
    grid_rows = devices // GC
    row_strip = device // GC
    col_strip = device % GC
    block_rows, slots, width, _ = tile_values.shape
    pair = STRIPS // 2

    strip_rows = lax.dynamic_slice_in_dim(tile_columns, row_strip * block_rows, block_rows, 0)
    far_first = 0
    if block_rows == pair * 2 * CB:
        far_first = pair * (col_strip // (pair * 2) != row_strip).astype(jnp.int32)
    order = jnp.bitwise_xor(jnp.arange(STRIPS, dtype=jnp.int32), far_first)
    strips = jnp.bitwise_xor(col_strip, 2 * order)
    own = jnp.take(strip_rows, col_strip, axis=1)
    match = own[:, :, None] == jnp.arange(PC, dtype=jnp.int32)
    slot = jnp.max(
        jnp.where(match, jnp.arange(slots, dtype=jnp.int32)[None, :, None], -1), axis=1
    )
    index = jnp.take(strip_rows, strips, axis=1)
    index = index + CB * (jnp.arange(STRIPS, dtype=jnp.int32) % pair)[None, :, None]
    index = index.reshape(-1)
    keep = keep_tiles.reshape(-1)
    relayed = grid_rows == 2 and block_rows == 2 * pair * CB
    unit = math.gcd(CB, block_rows)
    unit_rows = strips[:, None] * CB + unit * jnp.arange(CB // unit, dtype=jnp.int32)
    part = jnp.bitwise_xor(unit_rows // block_rows, row_strip)
    offset = unit_rows % block_rows
    if relayed:
        part, offset = offset // (2 * CB), offset % CB
    where = jnp.stack([part, offset], axis=-1).reshape(-1)
    half = len(where) // 2

    def shared(pieces):
        odd = col_strip % 2 == 1
        pieces = [p[r : r + CB] for p in pieces for r in range(0, p.shape[0], CB)]
        kept = [jnp.where(odd, b, a) for a, b in zip(pieces[::2], pieces[1::2])]
        given = [jnp.where(odd, a, b) for a, b in zip(pieces[::2], pieces[1::2])]
        return kept, [swapped(p, 1) for p in given]

    rows = block_rows // 16 or 1
    one, two = 8 * rows, 13 * rows
    if block_rows % 16:
        one, two = block_rows // 3, 2 * (block_rows // 3)
    few = one // 2 or one
    from_x = swapped(tile_values, 2)
    own, *panel = make_panel(tile_values, slot, 2 if relayed else 1, one)
    from_z = [swapped(own, 4)]
    if relayed:
        across = GC + GC // 2
        near = pack(where, 0, *shared(panel))
        crossed = [swapped(panel[0], across, inner)]
        crossed.append(swapped(after(panel[1], crossed[0]), across, inner))
        inward, outward = [], []
        middle_rows = tile_values[one:two]
        early = [near, middle_rows]
        for got, piece in zip(crossed, panel):
            ready = from_z + inward + outward + (early if inward else [])
            inward.append(swapped(after(piece, *ready), 4, outer))
            outward.append(swapped(after(got, *ready), 4, inner))
        returned = [swapped(after(inward[0], crossed[1]), across, inner)]
        last = jnp.concatenate([from_x[two:], tile_values[two:]])
        returned.append(swapped(after(inward[1], returned[0], last), across, inner))
        is_inner = inner(device)
        kept, received = [], []
        for a, b in zip(returned, outward):
            k, r = shared([jnp.where(is_inner, a, b)])
            kept += k
            received += r
        far = pack(where, half // 2, kept, received)
        tied = [inward[1], outward[1]]
    else:
        panels = panel
        for bit in range(low_bits, all_bits):
            panels = panels + [swapped(p, 1 << bit) for p in panels]
        others = [swapped(p, 1) for p in panels]
        near = pack(where, 0, panels, others)
        far = pack(where, half // 2, panels, others)
        tied = []
        middle_rows = tile_values[one:two]
        last = jnp.concatenate([from_x[two:], tile_values[two:]])
    from_xz = [swapped(after(from_z[0][:few], from_x), 2)]
    if few < one:
        from_xz.append(swapped(after(from_z[0][few:], from_xz[0]), 2))
    tied = tied + [from_xz[0], last, keep, index]
    from_z.append(swapped(after(middle_rows, *tied), 4))
    last = swapped(after(last, from_z[1], from_xz[-1]), 4)
    from_xz.append(swapped(after(from_z[1], from_xz[-1]), 2))

    def tiles_at(row):
        if row >= two:
            far_tiles = [(last, row - two + block_rows - two), (last, row - two)]
        elif row >= one:
            far_tiles = [(from_z[1], row - one), (from_xz[-1], row - one)]
        else:
            first = row < few
            far_tiles = [(from_z[0], row), (from_xz[0 if first else 1], row if first else row - few)]
        return [(tile_values, row), (from_x, row)] + far_tiles

    squared = None
    keep, index = lax.optimization_barrier((keep, index, from_z[1]))[:2]
    totals = []
    sums = jnp.zeros((8, PC * width), jnp.float32)
    for lo, hi in ((0, one), (one, two), (two, block_rows)):
        table = index
        if len(totals) == 2:
            table = after(index, totals[0], got[0])
        pieces = [tiles_at(row) for row in range(lo, hi, rows)]
        mine, other = expand(rows, lo, pieces, order, table, near, far)
        got = [swapped(a, 1) for a in other]
        squared, sums = square(keep, sums, mine, got, lo, block_rows, squared)
        totals.append(sums)
    for bit in range(low_bits, all_bits - 1):
        sums = sums + swapped(sums, 1 << bit)
    got = swapped(sums, 1 << (all_bits - 1))
    return scale(float(CB * GC * width), sums, got, squared)


def solution(mesh):
    return jax.shard_map(
        shards,
        mesh=mesh,
        in_specs=(
            P(("groups", "grid"), None, None, None),
            P("groups", None, None),
            P(("groups", "grid"), None),
        ),
        out_specs=P(("groups", "grid"), None, None, None),
        check_vma=False,
    )
```

```python
import functools
import math

import jax
import jax.numpy as jnp
from jax import lax
from jax.experimental import pallas as pl
from jax.experimental.pallas import tpu as pltpu
from jax.sharding import PartitionSpec as P

GC = 8
CB = 12
PC = CB // 4
STRIPS = GC // 2
MIB = 1 << 20
SHORT = pl.CostEstimate(flops=0, bytes_accessed=1024, transcendentals=0)


def swapped(array, mask, among=lambda i: True):
    pairs = [(i, i ^ mask) for i in range(lax.axis_size("grid")) if among(i)]
    return lax.ppermute(array, "grid", pairs)


def inner(i):
    return (i ^ i >> 1) & (GC // 2) != 0


def outer(i):
    return not inner(i)


def panel_kernel(first_steps, slot_ref, tiles_ref, first_ref, *panel_refs):
    rows, _, width, _ = tiles_ref.shape
    first = pl.program_id(0) * rows
    steps = pl.num_programs(0) // len(panel_refs)

    @pl.when(pl.program_id(0) < first_steps)
    def _():
        first_ref[...] = tiles_ref[...]

    for n, panel_ref in enumerate(panel_refs):

        @pl.when(pl.program_id(0) // steps == n)
        def _():
            @pl.loop(0, rows)
            def _(r):
                for p in range(PC):
                    slot = slot_ref[(first + r) * PC + p]
                    tile = tiles_ref[r, jnp.maximum(slot, 0)]
                    panel_ref[r, :, p * width : (p + 1) * width] = jnp.where(
                        slot >= 0, tile, jnp.zeros_like(tile)
                    )


def make_panel(tile_values, slots, parts, first_rows):
    block_rows, slots_per_row, width, _ = tile_values.shape
    part_rows = block_rows // parts
    step = math.gcd(math.gcd(part_rows, first_rows), 6)
    steps = part_rows // step
    first_steps = first_rows // step

    def part_block(n):
        return pl.BlockSpec(
            (step, width, PC * width), lambda i, s: (jnp.clip(i - n * steps, 0, steps - 1), 0, 0)
        )

    tile_shape = (slots_per_row, width, width)
    return pl.pallas_call(
        functools.partial(panel_kernel, first_steps),
        grid_spec=pltpu.PrefetchScalarGridSpec(
            num_scalar_prefetch=1,
            grid=(block_rows // step,),
            in_specs=[pl.BlockSpec((step, slots_per_row, width, width), lambda i, s: (i, 0, 0, 0))],
            out_specs=[
                pl.BlockSpec(
                    (step, *tile_shape), lambda i, s: (jnp.minimum(i, first_steps - 1), 0, 0, 0)
                )
            ]
            + [part_block(n) for n in range(parts)],
        ),
        out_shape=[jax.ShapeDtypeStruct((first_rows, *tile_shape), jnp.bfloat16)]
        + [jax.ShapeDtypeStruct((part_rows, width, PC * width), jnp.bfloat16)] * parts,
        compiler_params=pltpu.CompilerParams(vmem_limit_bytes=12 * MIB),
        cost_estimate=SHORT,
        name="panel",
    )(slots.reshape(-1), tile_values)


def pack_kernel(first, parts, where_ref, *refs):
    sources, packed_ref, sem = refs[: 2 * parts], refs[-2], refs[-1]
    part_rows, _, half = sources[0].shape
    unit = math.gcd(CB, part_rows)
    for n in range(packed_ref.shape[0] // unit):
        part = where_ref[2 * (first + n)]
        offset = where_ref[2 * (first + n) + 1]
        for m in range(parts):

            @pl.when((part == m) | (parts == 1))
            def _():
                for side in range(2):
                    pltpu.make_async_copy(
                        sources[side * parts + m].at[pl.ds(offset, unit)],
                        packed_ref.at[pl.ds(n * unit, unit), :, pl.ds(side * half, half)],
                        sem.at[side],
                    ).start()
    for side in range(2):
        cols = pl.ds(side * half, half)
        pltpu.make_async_copy(
            packed_ref.at[:, :, cols], packed_ref.at[:, :, cols], sem.at[side]
        ).wait()


def pack(where, first, mine, others):
    parts = len(mine)
    _, width, half = mine[0].shape
    return pl.pallas_call(
        functools.partial(pack_kernel, first, parts),
        out_shape=jax.ShapeDtypeStruct((STRIPS // 2 * CB, width, 2 * half), jnp.bfloat16),
        in_specs=[pl.BlockSpec(memory_space=pltpu.SMEM)]
        + [pl.BlockSpec(memory_space=pl.ANY)] * (2 * parts),
        out_specs=pl.BlockSpec(memory_space=pltpu.VMEM),
        scratch_shapes=[pltpu.SemaphoreType.DMA((2,))],
        compiler_params=pltpu.CompilerParams(vmem_limit_bytes=8 * MIB),
        cost_estimate=SHORT,
        name="pack",
    )(where, *mine, *others)


def expand_kernel(first, plan, order_ref, index_ref, near_ref, far_ref, *refs):
    steps = len(plan)
    outs, (tiles, sums, tile_sem, sum_sem) = refs[-5 - steps : -4], refs[-4:]
    mine_ref, other_refs = outs[0], outs[1:]
    _, _, rows, slots, width, _ = tiles.shape
    half = PC * width
    total_rows = steps * rows

    def fetch(k):
        return [
            pltpu.make_async_copy(
                refs[source].at[pl.ds(offset, rows)], tiles.at[k % 2, q], tile_sem.at[k % 2, q]
            )
            for q, (source, offset) in enumerate(plan[k])
        ]

    def stores(k, r, slot):
        targets = (mine_ref.at[k * rows + r], other_refs[k].at[r])
        return [
            pltpu.make_async_copy(
                sums.at[slot, :, pl.ds(side * half, half)], target, sum_sem.at[slot, side]
            )
            for side, target in enumerate(targets)
        ]

    for copy in fetch(0):
        copy.start()
    for k in range(steps):
        if k + 1 < steps:
            for copy in fetch(k + 1):
                copy.start()
        for copy in fetch(k):
            copy.wait()

        @pl.loop(0, rows)
        def _(r):
            row = k * rows + r
            slot = lax.rem(row, 2)

            @pl.when(row >= 2)
            def _():
                for copy in stores(k, r, slot):
                    copy.wait()

            total = None
            for n in range(STRIPS):
                panel = near_ref if n < STRIPS // 2 else far_ref
                q = order_ref[n]
                for t in range(0, slots, 2):
                    base = (first + row) * (STRIPS * slots) + n * slots + t
                    left = jnp.concatenate(
                        [tiles[k % 2, q, r, t], tiles[k % 2, q, r, t + 1]], axis=1
                    )
                    right = jnp.concatenate(
                        [panel[index_ref[base]], panel[index_ref[base + 1]]], axis=0
                    )
                    term = jnp.dot(left, right, preferred_element_type=jnp.float32)
                    total = term if total is None else total + term
            sums[slot] = total
            for copy in stores(k, r, slot):
                copy.start()

    for row in range(max(total_rows - 2, 0), total_rows):
        for copy in stores(row // rows, row % rows, row % 2):
            copy.wait()


def expand(rows, first, pieces, order, index, near, far):
    arrays = []
    plan = []
    for piece in pieces:
        for array, _ in piece:
            if all(array is not a for a in arrays):
                arrays.append(array)
        plan.append([([array is a for a in arrays].index(True), row) for array, row in piece])
    _, slots, width, _ = arrays[0].shape
    half = PC * width
    anywhere = pl.BlockSpec(memory_space=pl.ANY)
    smem = pl.BlockSpec(memory_space=pltpu.SMEM)
    vmem = pl.BlockSpec(memory_space=pltpu.VMEM)
    out = pl.pallas_call(
        functools.partial(expand_kernel, first, plan),
        out_shape=[jax.ShapeDtypeStruct((len(plan) * rows, width, half), jnp.float32)]
        + [jax.ShapeDtypeStruct((rows, width, half), jnp.float32)] * len(plan),
        in_specs=[smem, smem, vmem, vmem] + [anywhere] * len(arrays),
        out_specs=[pl.BlockSpec(memory_space=pltpu.HBM)] * (1 + len(plan)),
        scratch_shapes=[
            pltpu.VMEM((2, STRIPS, rows, slots, width, width), jnp.bfloat16),
            pltpu.VMEM((2, width, 2 * half), jnp.float32),
            pltpu.SemaphoreType.DMA((2, STRIPS)),
            pltpu.SemaphoreType.DMA((2, 2)),
        ],
        compiler_params=pltpu.CompilerParams(vmem_limit_bytes=12 * MIB),
        cost_estimate=SHORT,
        name="expand",
    )(order, index, near, far, *arrays)
    return out[0], out[1:]


def square_kernel(lo, pieces, keep_ref, before_ref, mine_ref, *refs):
    got_refs, (squared_ref, sums_ref) = refs[:pieces], refs[-2:]
    rows, width, _ = mine_ref.shape
    first = lo + pl.program_id(0) * rows

    @pl.when(pl.program_id(0) == 0)
    def _():
        sums_ref[...] = before_ref[...]

    for n, got_ref in enumerate(got_refs):

        @pl.when(pl.program_id(0) == n)
        def _():
            @pl.loop(0, rows)
            def _(r):
                for p in range(PC):
                    keep = keep_ref[(first + r) * PC + p].astype(jnp.float32)
                    cols = slice(p * width, (p + 1) * width)
                    value = mine_ref[r, :, cols] + got_ref[r, :, cols]
                    value = value * value * keep
                    squared_ref[r, :, cols] = value
                    sums_ref[:, cols] += jnp.sum(value.reshape(width // 8, 8, width), axis=0)


def square(keep, before, mine, got, lo, total_rows, buffer):
    _, width, half = mine.shape
    step = got[0].shape[0]
    block = pl.BlockSpec((step, width, half), lambda i, s: (i, 0, 0))
    whole = pl.BlockSpec((step, width, half), lambda i, s: (0, 0, 0))
    target = pl.BlockSpec((step, width, half), lambda i, s: (lo // step + i, 0, 0))
    sums = pl.BlockSpec((8, half), lambda i, s: (0, 0))
    operands = [keep, before, mine, *got]
    in_specs = [sums, block] + [whole] * len(got)
    aliases = {}
    if buffer is not None:
        operands.append(buffer)
        in_specs.append(pl.BlockSpec(memory_space=pl.ANY))
        aliases = {len(operands) - 1: 0}
    return pl.pallas_call(
        functools.partial(square_kernel, lo, len(got)),
        grid_spec=pltpu.PrefetchScalarGridSpec(
            num_scalar_prefetch=1,
            grid=(len(got),),
            in_specs=in_specs,
            out_specs=(target, sums),
        ),
        out_shape=(
            jax.ShapeDtypeStruct((total_rows, width, half), jnp.float32),
            jax.ShapeDtypeStruct((8, half), jnp.float32),
        ),
        input_output_aliases=aliases,
        compiler_params=pltpu.CompilerParams(vmem_limit_bytes=20 * MIB),
        cost_estimate=SHORT,
        name="square",
    )(*operands)


def scale_kernel(count, sums_ref, got_ref, squared_ref, out_ref):
    step, width, _ = squared_ref.shape
    for p in range(PC):
        cols = slice(p * width, (p + 1) * width)
        sums = jnp.sum(sums_ref[:, cols] + got_ref[:, cols], axis=0, keepdims=True)
        inverse = 1.0 / (sums / count + 1e-6)
        for r in range(step):
            out_ref[r, p] = squared_ref[r, :, cols] * inverse


def scale(count, sums, got, squared):
    rows, width, half = squared.shape
    step = math.gcd(rows, 6)
    return pl.pallas_call(
        functools.partial(scale_kernel, count),
        grid=(rows // step,),
        in_specs=[pl.BlockSpec((8, half), lambda i: (0, 0))] * 2
        + [pl.BlockSpec((step, width, half), lambda i: (i, 0, 0))],
        out_specs=pl.BlockSpec((step, PC, width, width), lambda i: (i, 0, 0, 0)),
        out_shape=jax.ShapeDtypeStruct((rows, PC, width, width), jnp.float32),
        compiler_params=pltpu.CompilerParams(vmem_limit_bytes=12 * MIB),
        cost_estimate=SHORT,
        name="scale",
    )(sums, got, squared)


def after(array, *earlier):
    return lax.optimization_barrier((array, *earlier))[0]


def shards(tile_values, tile_columns, keep_tiles):
    devices = lax.axis_size("grid")
    device = lax.axis_index("grid")
    all_bits = devices.bit_length() - 1
    low_bits = GC.bit_length() - 1
    grid_rows = devices // GC
    row_strip = device // GC
    col_strip = device % GC
    block_rows, slots, width, _ = tile_values.shape
    pair = STRIPS // 2

    strip_rows = lax.dynamic_slice_in_dim(tile_columns, row_strip * block_rows, block_rows, 0)
    far_first = 0
    if block_rows == pair * 2 * CB:
        far_first = pair * (col_strip // (pair * 2) != row_strip).astype(jnp.int32)
    order = jnp.bitwise_xor(jnp.arange(STRIPS, dtype=jnp.int32), far_first)
    strips = jnp.bitwise_xor(col_strip, 2 * order)
    own = jnp.take(strip_rows, col_strip, axis=1)
    match = own[:, :, None] == jnp.arange(PC, dtype=jnp.int32)
    slot = jnp.max(
        jnp.where(match, jnp.arange(slots, dtype=jnp.int32)[None, :, None], -1), axis=1
    )
    index = jnp.take(strip_rows, strips, axis=1)
    index = index + CB * (jnp.arange(STRIPS, dtype=jnp.int32) % pair)[None, :, None]
    index = index.reshape(-1)
    keep = keep_tiles.reshape(-1)
    relayed = grid_rows == 2 and block_rows == 2 * pair * CB
    unit = math.gcd(CB, block_rows)
    unit_rows = strips[:, None] * CB + unit * jnp.arange(CB // unit, dtype=jnp.int32)
    part = jnp.bitwise_xor(unit_rows // block_rows, row_strip)
    offset = unit_rows % block_rows
    if relayed:
        part, offset = offset // (2 * CB), offset % CB
    where = jnp.stack([part, offset], axis=-1).reshape(-1)
    half = len(where) // 2

    def shared(pieces):
        odd = col_strip % 2 == 1
        pieces = [p[r : r + CB] for p in pieces for r in range(0, p.shape[0], CB)]
        kept = [jnp.where(odd, b, a) for a, b in zip(pieces[::2], pieces[1::2])]
        given = [jnp.where(odd, a, b) for a, b in zip(pieces[::2], pieces[1::2])]
        return kept, [swapped(p, 1) for p in given]

    rows = block_rows // 16 or 1
    one, two = 8 * rows, 13 * rows
    if block_rows % 16:
        one, two = block_rows // 3, 2 * (block_rows // 3)
    few = one // 2 or one
    from_x = swapped(tile_values, 2)
    own, *panel = make_panel(tile_values, slot, 2 if relayed else 1, one)
    from_z = [swapped(own, 4)]
    if relayed:
        across = GC + GC // 2
        near = pack(where, 0, *shared(panel))
        crossed = [swapped(panel[0], across, inner)]
        crossed.append(swapped(after(panel[1], crossed[0]), across, inner))
        inward, outward = [], []
        middle_rows = tile_values[one:two]
        early = [near, middle_rows]
        for got, piece in zip(crossed, panel):
            ready = from_z + inward + outward + (early if inward else [])
            inward.append(swapped(after(piece, *ready), 4, outer))
            outward.append(swapped(after(got, *ready), 4, inner))
        returned = [swapped(after(inward[0], crossed[1]), across, inner)]
        last = jnp.concatenate([from_x[two:], tile_values[two:]])
        returned.append(swapped(after(inward[1], returned[0], last), across, inner))
        is_inner = inner(device)
        kept, received = [], []
        for a, b in zip(returned, outward):
            k, r = shared([jnp.where(is_inner, a, b)])
            kept += k
            received += r
        far = pack(where, half // 2, kept, received)
        tied = [inward[1], outward[1]]
    else:
        panels = panel
        for bit in range(low_bits, all_bits):
            panels = panels + [swapped(p, 1 << bit) for p in panels]
        others = [swapped(p, 1) for p in panels]
        near = pack(where, 0, panels, others)
        far = pack(where, half // 2, panels, others)
        tied = []
        middle_rows = tile_values[one:two]
        last = jnp.concatenate([from_x[two:], tile_values[two:]])
    from_xz = [swapped(after(from_z[0][:few], from_x), 2)]
    if few < one:
        from_xz.append(swapped(after(from_z[0][few:], from_xz[0]), 2))
    tied = tied + [from_xz[0], last, keep, index]
    from_z.append(swapped(after(middle_rows, *tied), 4))
    last = swapped(after(last, from_z[1], from_xz[-1]), 4)
    from_xz.append(swapped(after(from_z[1], from_xz[-1]), 2))

    def tiles_at(row):
        if row >= two:
            far_tiles = [(last, row - two + block_rows - two), (last, row - two)]
        elif row >= one:
            far_tiles = [(from_z[1], row - one), (from_xz[-1], row - one)]
        else:
            first = row < few
            far_tiles = [(from_z[0], row), (from_xz[0 if first else 1], row if first else row - few)]
        return [(tile_values, row), (from_x, row)] + far_tiles

    squared = None
    keep, index = lax.optimization_barrier((keep, index, from_z[1]))[:2]
    totals = []
    sums = jnp.zeros((8, PC * width), jnp.float32)
    for lo, hi in ((0, one), (one, two), (two, block_rows)):
        table = index
        if len(totals) == 2:
            table = after(index, totals[0], got[0])
        pieces = [tiles_at(row) for row in range(lo, hi, rows)]
        mine, other = expand(rows, lo, pieces, order, table, near, far)
        got = [swapped(a, 1) for a in other]
        squared, sums = square(keep, sums, mine, got, lo, block_rows, squared)
        totals.append(sums)
    for bit in range(low_bits, all_bits - 1):
        sums = sums + swapped(sums, 1 << bit)
    got = swapped(sums, 1 << (all_bits - 1))
    return scale(float(CB * GC * width), sums, got, squared)


def solution(mesh):
    return jax.shard_map(
        shards,
        mesh=mesh,
        in_specs=(
            P(("groups", "grid"), None, None, None),
            P("groups", None, None),
            P(("groups", "grid"), None),
        ),
        out_specs=P(("groups", "grid"), None, None, None),
        check_vma=False,
    )
```
